256 devices in a mesh: row: 32 (over z, y_hi, core), col: 8 (over x, y_lo).
Axes of the slice: x: 4, y: 4 (y_hi: 2, y_lo: 2; y = y_hi * 2 + y_lo), z: 8, core: 2. Of those that a mesh axis runs over, the one named last changes fastest.
Arguments:
- activations: bfloat16 [1024, 8192], P('col', 'row'), may hold values from -0.1875 to 0.1875
- out_grad: bfloat16 [1024, 32768], P('row', 'col'), may hold values from -6 to 6
- weight: bfloat16 [8192, 32768], P('row', 'col'), may hold values from -0.03125 to 0.03125
Outputs:
- input_grad: bfloat16 [1024, 8192], P('col', 'row')
- weight_grad: bfloat16 [8192, 32768], P('row', 'col')
- left_stats: float32 [32, 8, 1, 1024, 1024], P('row', 'col')
- right_stats: float32 [32, 8, 1, 1024, 1024], P('row', 'col')
The draws below stay inside these ranges and needn't reach their ends.
All inputs are finite; a program needn't handle non-finite values.
Results may differ from the reference program's by a relative error of at most 0.0034.
Values may be sent and summed in bfloat16 or wider, within the bound.
A program may use at most 64 MiB of HBM per device.

```python
import jax
import jax.numpy as jnp
from jax import lax

D = 8192
F = 32768
BLK = 1024
TOKENS = 1024
GROUP = 4
CBLK = 4
PER = 1
N_ROW = 32
N_COL = 8


def with_spikes(drawn, rng, source, target, parts, factor):
    owner, partner = [(jnp.arange(drawn.shape[axis_at]) // (drawn.shape[axis_at] // parts)).reshape([-1 if axis == axis_at else 1 for axis in range(drawn.ndim)]) for axis_at in (source, target)]
    chosen = jax.random.permutation(rng, parts)[partner]
    strong = (owner == chosen) | (owner == (partner + parts // 2) % parts)
    return jnp.where(strong, factor * drawn, drawn)


def steps_of(key, dims, pieces, low, top_value):
    factor_of, own = 1.0, jax.random.fold_in(key, 6)
    for position, parts in pieces:
        steps = jnp.exp(jax.random.uniform(jax.random.fold_in(own, position), (parts,), jnp.float32, low / len(pieces), top_value / len(pieces)))
        factor_of = factor_of * jnp.repeat(steps, dims[position] // parts).reshape([-1 if axis == position else 1 for axis in range(len(dims))])
    return factor_of


def centred(own_key, extent, width, most, pieces=(), kind=jnp.bfloat16):
    values = width * jax.random.normal(own_key, extent, jnp.float32)
    if pieces:
        values = values * steps_of(own_key, extent, pieces, -0.22, 0.18)
    return jnp.clip(values, -most, most).astype(kind)


def heavy_noise(rng, shape, spread, bound, shards, heavy, kind=jnp.bfloat16):
    drawn = spread * jax.random.normal(rng, shape, jnp.float32)
    if shards:
        drawn = drawn * steps_of(rng, shape, shards, -0.22, 0.18)
    return jnp.clip(with_spikes(drawn, jax.random.fold_in(rng, 3), *heavy), -bound, bound).astype(kind)


def setup_inputs(seed: int = 0) -> dict:
    seeds = jax.random.split(jax.random.key(seed), 4)
    activations = centred(seeds[0], (TOKENS, D), 0.03125, 0.1875, ((0, 8), (1, 32)))
    out_grad = heavy_noise(seeds[1], (TOKENS, F), 1.0, 6.0, ((0, 32), (1, 8)), (1, 0, 32, 2.75))
    weight = centred(seeds[2], (D, F), F ** -0.5, 0.03125, ((0, 32), (1, 8)))
    return dict(activations=activations, out_grad=out_grad, weight=weight)


def reference(activations, out_grad, weight):
    weight_grad = jnp.dot(activations.T, out_grad, preferred_element_type=jnp.float32).astype(jnp.bfloat16)
    input_grad = jnp.dot(out_grad, weight.T, preferred_element_type=jnp.float32).astype(jnp.bfloat16)

    def block_stats(entry):
        row_index = entry // (N_COL * PER)
        col_index = (entry // PER) % N_COL
        sub_index = entry % PER
        row_start = (BLK * (row_index // GROUP)).astype(jnp.int32)
        col_start = (BLK * (col_index * CBLK + (row_index % GROUP) * PER + sub_index)).astype(jnp.int32)
        weight_block = lax.dynamic_slice(weight_grad, (row_start, col_start), (BLK, BLK))
        left_gram = jnp.dot(weight_block, weight_block.T, preferred_element_type=jnp.float32) * (1.0 / BLK)
        right_gram = jnp.dot(weight_block.T, weight_block, preferred_element_type=jnp.float32) * (1.0 / BLK)
        return left_gram, right_gram

    entries = jnp.arange(N_ROW * N_COL * PER, dtype=jnp.int32)
    left_all, right_all = lax.map(block_stats, entries)
    left_stats = left_all.reshape(N_ROW, N_COL, PER, BLK, BLK)
    right_stats = right_all.reshape(N_ROW, N_COL, PER, BLK, BLK)
    return input_grad, weight_grad, left_stats, right_stats
```

```python
import functools

import jax
import jax.numpy as jnp
from jax import lax
from jax.experimental import pallas as pl
from jax.experimental.pallas import tpu as pltpu
from jax.sharding import PartitionSpec as P

MESH = pl.DeviceIdType.MESH
F32 = jnp.float32
BF16 = jnp.bfloat16


def gather_kernel(
    acts_ref, og_ref, w_ref,
    ig_ref, wg_ref, g_ref,
    panel, w_v, acts, wacc, gacc, stage, inbox,
    local_sem, zsend, zrecv, ysend, yrecv, msend, mrecv,
    aysend, ayrecv, asend, arecv, amsend, amrecv, rsend, rrecv,
):
    row, col = lax.axis_index("row"), lax.axis_index("col")
    z, line, core = row // 4, lax.rem(row // 2, 2), lax.rem(row, 2)
    member = 2 * line + core
    half = og_ref.shape[1] // 2
    quarter = og_ref.shape[1] // 4
    up = (lax.rem(z + 1, 8) * 4 + member, col)
    down = (lax.rem(z + 7, 8) * 4 + member, col)
    across = (z * 4 + 2 * (1 - line) + core, col)
    mate = (z * 4 + 2 * line + 1 - core, col)

    def peer(step):
        return (row, lax.rem(col + step, 8))

    def remote(src, dst, send, recv, device):
        return pltpu.make_async_remote_copy(
            src_ref=src, dst_ref=dst, send_sem=send, recv_sem=recv,
            device_id=device, device_id_type=MESH,
        )

    barrier = pltpu.get_barrier_semaphore()
    for device in [up, down, across, mate] + [peer(step) for step in range(1, 8)]:
        pl.semaphore_signal(barrier, inc=1, device_id=device, device_id_type=MESH)
    pl.semaphore_wait(barrier, 11)

    def plane(distance, way):
        return lax.rem(z + 8 - distance if way == 0 else z + distance, 8)

    def block(where, of_partner, other_core=False):
        which = 1 - line if of_partner else line
        return where * 4 + 2 * which + (1 - core if other_core else core)

    def zref(ref, step, way):
        if step < 4:
            return ref
        return ref.at[:, pl.ds(way * half, half)]

    def zcopy(of_partner, step, way):
        index = block(plane(step - 1, way), of_partner)
        source = og_ref if step == 1 and not of_partner else panel.at[index]
        slot = (way, int(of_partner), step - 1)
        return remote(
            zref(source, step, way), zref(panel.at[index], step, way),
            zsend.at[slot], zrecv.at[slot], up if way == 0 else down,
        )

    def zarrive(of_partner, step, way):
        index = block(plane(step, way), of_partner)
        here = zref(panel.at[index], step, way)
        slot = (way, int(of_partner), step - 1)
        remote(here, here, zsend.at[slot], zrecv.at[slot], up if way == 0 else down).wait_recv()

    def to_mate(where, of_partner, source=None):
        index = block(where, of_partner)
        slot = where * 2 + (1 - line if of_partner else line)
        return remote(
            panel.at[index] if source is None else source, panel.at[index],
            msend.at[slot], mrecv.at[slot], mate,
        )

    def from_mate(where, of_partner):
        index = block(where, of_partner, True)
        slot = where * 2 + (1 - line if of_partner else line)
        here = panel.at[index]
        remote(here, here, msend.at[slot], mrecv.at[slot], mate).wait_recv()

    for way in range(2):
        zcopy(False, 1, way).start()
    to_across = remote(og_ref, panel.at[row], ysend, yrecv, across)
    to_across.start()
    to_mate(z, False, og_ref).start()
    own_copy = pltpu.make_async_copy(og_ref, panel.at[row], local_sem.at[0])
    own_copy.start()
    w_copy = pltpu.make_async_copy(w_ref, w_v, local_sem.at[1])
    w_copy.start()

    acts[core, col, line] = acts_ref[...].astype(F32).T.astype(BF16)
    mine = acts.at[core, col, line]
    act_across = remote(mine, mine, aysend, ayrecv, across)
    act_across.start()
    other = acts.at[core, col, 1 - line]
    remote(other, other, aysend, ayrecv, across).wait_recv()
    pair = acts.at[core, col]

    def act_send(step):
        return remote(pair, pair, asend.at[step], arecv.at[col], peer(step))

    def act_mate(where):
        ref = acts.at[core, where]
        return remote(ref, ref, amsend.at[where], amrecv.at[where], mate)

    for step in range(1, 8):
        act_send(step).start()
    act_mate(col).start()

    def forward(of_partner, step):
        for way in range(2):
            zarrive(of_partner, step, way)
            if step < 4:
                zcopy(of_partner, step + 1, way).start()
                to_mate(plane(step, way), of_partner).start()
        if step == 4:
            to_mate(plane(4, 0), of_partner).start()

    def chunk(where, columns):
        return panel[pl.ds(where * 4, 4), :, columns].reshape(128, columns.size)

    def input_grad(planes):
        tokens = 128 * len(planes)

        def add(k, total):
            columns = pl.ds(pl.multiple_of(k * quarter, quarter), quarter)
            lhs = jnp.concatenate([chunk(where, columns) for where in planes], axis=0)
            return total + lax.dot_general(
                lhs, w_v[:, columns], (((1,), (1,)), ((), ())), preferred_element_type=F32
            )

        total = lax.fori_loop(0, 4, add, jnp.zeros((tokens, w_v.shape[0]), F32))
        for i, where in enumerate(planes):
            stage[where] = total[i * 128:(i + 1) * 128]

            @pl.when(where != col)
            def _():
                sum_send(where).start()

    def sum_send(where):
        return remote(stage.at[where], inbox.at[col], rsend.at[where], rrecv.at[col], (row, where))

    def weight_grad(planes, first=False, last=False):
        def lhs_of(of_core, of_line):
            return jnp.concatenate([acts[of_core, where, of_line] for where in planes], axis=1)

        def rhs_of(columns):
            return jnp.concatenate([chunk(where, columns) for where in planes], axis=0)

        def own(t, carry):
            columns = pl.ds(pl.multiple_of(t * 512, 512), 512)
            out = jnp.dot(lhs_of(core, line), rhs_of(columns), preferred_element_type=F32)
            if not first:
                out = out + wacc[:, columns]
            if last:
                wg_ref[:, columns] = out.astype(BF16)
            else:
                wacc[:, columns] = out
            return carry

        lax.fori_loop(0, 8, own, 0)

        def others(t, carry):
            which = lax.rem(member + 1 + t // 2, 4)
            columns = pl.ds(pl.multiple_of(member * quarter + lax.rem(t, 2) * 512, 512), 512)
            place = pl.ds(pl.multiple_of(lax.rem(t, 2) * 512, 512), 512)
            out = jnp.dot(
                lhs_of(lax.rem(which, 2), which // 2), rhs_of(columns), preferred_element_type=F32
            )
            if not first:
                out = out + gacc[which, :, place]
            if last:
                g_ref[which, :, place] = out.astype(BF16)
            else:
                gacc[which, :, place] = out
            return carry

        lax.fori_loop(0, 6, others, 0)

    def both(step):
        return [plane(step, 0), plane(step, 1)]

    def from_mate_all(planes):
        for where in planes:
            from_mate(where, False)
            from_mate(where, True)

    forward(False, 1)
    here = panel.at[block(z, True)]
    remote(here, here, ysend, yrecv, across).wait_recv()
    for way in range(2):
        zcopy(True, 1, way).start()
    to_mate(z, True).start()
    own_copy.wait()
    w_copy.wait()
    from_mate_all([z])
    input_grad([z])

    def act_forward(step, carry):
        where = lax.rem(col + step, 8)
        ref = acts.at[core, where]
        remote(ref, ref, asend.at[step], arecv.at[where], mate).wait_recv()
        act_mate(where).start()
        return carry

    forward(False, 2)
    lax.fori_loop(1, 8, act_forward, 0)
    forward(True, 1)
    from_mate_all(both(1))
    input_grad(both(1))

    def act_from_mate(where, carry):
        ref = acts.at[1 - core, where]
        remote(ref, ref, amsend.at[where], amrecv.at[where], mate).wait_recv()
        return carry

    lax.fori_loop(0, 8, act_from_mate, 0)
    forward(False, 3)
    weight_grad(both(1), first=True)
    forward(True, 2)
    from_mate_all(both(2))
    input_grad(both(2))
    forward(False, 4)
    weight_grad(both(2))
    forward(True, 3)
    from_mate_all(both(3))
    input_grad(both(3))
    weight_grad(both(3))
    forward(True, 4)
    from_mate_all([plane(4, 0)])
    input_grad([plane(4, 0)])
    weight_grad([z, plane(4, 0)], last=True)
    g_ref[member] = wg_ref[:, pl.ds(pl.multiple_of(member * quarter, quarter), quarter)]

    def take(step, total):
        where = lax.rem(col + step, 8)
        ref = inbox.at[where]
        remote(ref, ref, rsend.at[where], rrecv.at[where], (row, where)).wait_recv()
        return total + inbox[where]

    ig_ref[...] = lax.fori_loop(1, 8, take, stage[col]).astype(BF16)

    for way in range(2):
        for of_partner in (False, True):
            for step in range(1, 5):
                zcopy(of_partner, step, way).wait_send()
    to_across.wait_send()
    act_across.wait_send()

    def drain(where, carry):
        for of_line in range(2):
            index = where * 4 + 2 * of_line + core
            slot = where * 2 + of_line
            ref = panel.at[index]
            remote(ref, ref, msend.at[slot], mrecv.at[slot], mate).wait_send()
        act_mate(where).wait_send()
        return carry

    lax.fori_loop(0, 8, drain, 0)

    def drain_peers(step, carry):
        act_send(step).wait_send()
        sum_send(lax.rem(col + step, 8)).wait_send()
        return carry

    lax.fori_loop(1, 8, drain_peers, 0)


def gram_kernel(g_ref, wg_in, left_ref, right_ref, wg_out):
    i = pl.program_id(0)
    size = left_ref.shape[0]
    rows = pl.ds(pl.multiple_of(i * size, size), size)
    wg_out[...] = wg_in[...]
    scale = 1.0 / g_ref.shape[0]
    left_ref[...] = scale * lax.dot_general(
        g_ref[rows, :], g_ref[...], (((1,), (1,)), ((), ())), preferred_element_type=F32
    )
    right_ref[...] = scale * lax.dot_general(
        g_ref[:, rows], g_ref[...], (((0,), (0,)), ((), ())), preferred_element_type=F32
    )


def on_device(activations, out_grad, weight):
    tokens, feats = activations.shape
    rows, cols = weight.shape
    vmem = pl.BlockSpec(memory_space=pltpu.VMEM)
    anywhere = pl.BlockSpec(memory_space=pl.ANY)
    dma = pltpu.SemaphoreType.DMA
    quarter = cols // 4
    input_grad, weight_grad, blocks = pl.pallas_call(
        gather_kernel,
        out_shape=(
            jax.ShapeDtypeStruct((tokens, feats), BF16),
            jax.ShapeDtypeStruct((rows, cols), BF16),
            jax.ShapeDtypeStruct((4, rows, quarter), BF16),
        ),
        in_specs=[vmem, anywhere, anywhere],
        out_specs=(vmem, vmem, vmem),
        scratch_shapes=[
            pltpu.VMEM((32, out_grad.shape[0], cols), BF16),
            pltpu.VMEM((rows, cols), BF16),
            pltpu.VMEM((2, 8, 2, feats, tokens), BF16),
            pltpu.VMEM((rows, cols), F32),
            pltpu.VMEM((4, rows, quarter), F32),
            pltpu.VMEM((8, tokens, feats), F32),
            pltpu.VMEM((8, tokens, feats), F32),
            dma((2,)),
            dma((2, 2, 4)), dma((2, 2, 4)), dma, dma, dma((16,)), dma((16,)),
            dma, dma, dma((8,)), dma((8,)), dma((8,)), dma((8,)), dma((8,)), dma((8,)),
        ],
        compiler_params=pltpu.CompilerParams(
            collective_id=0, has_side_effects=True, vmem_limit_bytes=44 * 2**20
        ),
        name="gather_and_grads",
    )(activations, out_grad, weight)

    size = 4 * rows
    step = size // 4
    left, right, weight_grad = pl.pallas_call(
        gram_kernel,
        grid=(4,),
        out_shape=(
            jax.ShapeDtypeStruct((size, quarter), F32),
            jax.ShapeDtypeStruct((quarter, quarter), F32),
            jax.ShapeDtypeStruct((rows, cols), BF16),
        ),
        in_specs=[
            pl.BlockSpec((size, quarter), lambda i: (0, 0)),
            pl.BlockSpec((rows // 4, cols), lambda i: (i, 0)),
        ],
        out_specs=(
            pl.BlockSpec((step, quarter), lambda i: (i, 0)),
            pl.BlockSpec((step, quarter), lambda i: (i, 0)),
            pl.BlockSpec((rows // 4, cols), lambda i: (i, 0)),
        ),
        compiler_params=pltpu.CompilerParams(vmem_limit_bytes=32 * 2**20),
        name="grams",
    )(blocks.reshape(size, quarter), weight_grad)
    return (
        input_grad,
        weight_grad,
        left.reshape(1, 1, 1, size, quarter),
        right.reshape(1, 1, 1, quarter, quarter),
    )


def solution(mesh):
    return jax.shard_map(
        on_device,
        mesh=mesh,
        in_specs=(P("col", "row"), P("row", "col"), P("row", "col")),
        out_specs=(
            P("col", "row"),
            P("row", "col"),
            P("row", "col", None, None, None),
            P("row", "col", None, None, None),
        ),
        check_vma=False,
    )
```

```python
import functools

import jax
import jax.numpy as jnp
from jax import lax
from jax.experimental import pallas as pl
from jax.experimental.pallas import tpu as pltpu
from jax.sharding import PartitionSpec as P

MESH = pl.DeviceIdType.MESH
F32 = jnp.float32
BF16 = jnp.bfloat16


def gather_kernel(
    acts_ref, og_ref, w_ref,
    ig_ref, wg_ref, g_ref,
    panel, w_v, acts_v, acts, wacc, gacc, wide, wide_in, slim, slim_in,
    local_sem, zsend, zrecv, ysend, yrecv, msend, mrecv,
    aysend, ayrecv, axsend, axrecv, amsend, amrecv, rsend, rrecv,
):
    row, col = lax.axis_index("row"), lax.axis_index("col")
    z, line, core = row // 4, lax.rem(row // 2, 2), lax.rem(row, 2)
    x, side = col // 2, lax.rem(col, 2)
    member = 2 * line + core
    half = og_ref.shape[1] // 2
    quarter = og_ref.shape[1] // 4
    up = (lax.rem(z + 1, 8) * 4 + member, col)
    down = (lax.rem(z + 7, 8) * 4 + member, col)
    far_row = z * 4 + 2 * (1 - line) + core
    across = (far_row, col)
    mate = (z * 4 + 2 * line + 1 - core, col)
    beside = (row, x * 2 + 1 - side)
    corner = (far_row, x * 2 + 1 - side)

    def x_peer(step, other=False):
        return (row, lax.rem(x + step, 4) * 2 + (1 - side if other else side))

    def remote(src, dst, send, recv, device):
        return pltpu.make_async_remote_copy(
            src_ref=src, dst_ref=dst, send_sem=send, recv_sem=recv,
            device_id=device, device_id_type=MESH,
        )

    act_copy = pltpu.make_async_copy(acts_ref, acts_v, local_sem.at[2])
    act_copy.start()
    barrier = pltpu.get_barrier_semaphore()
    peers = [up, down, across, mate, beside, corner]
    peers += [x_peer(step) for step in range(1, 4)] + [x_peer(step, True) for step in range(1, 4)]
    for device in peers:
        pl.semaphore_signal(barrier, inc=1, device_id=device, device_id_type=MESH)
    pl.semaphore_wait(barrier, len(peers))

    def plane(distance, way):
        return lax.rem(z + 8 - distance if way == 0 else z + distance, 8)

    def part(ref, which):
        return ref.at[:, pl.ds(which * half, half)]

    def block(where, of_partner):
        return panel.at[where * 4 + 2 * (1 - line if of_partner else line) + core]

    def zcopy(of_partner, step, way, which):
        slot = (way, int(of_partner), step - 1, which)
        target = block(plane(step - 1, way), of_partner)
        source = og_ref if step == 1 else target
        return remote(
            part(source, which), part(target, which),
            zsend.at[slot], zrecv.at[slot], up if way == 0 else down,
        )

    def zwait(of_partner, step, way, which):
        slot = (way, int(of_partner), step - 1, which)
        here = part(block(plane(step, way), of_partner), which)
        remote(here, here, zsend.at[slot], zrecv.at[slot], up if way == 0 else down).wait_recv()

    def yplane(slot):
        return (z, plane(1, 0), plane(1, 1), plane(4, 0))[slot]

    def ycopy(slot, which):
        target = block(yplane(slot), False)
        source = og_ref if slot == 0 else target
        return remote(
            part(source, which), part(target, which),
            ysend.at[slot, which], yrecv.at[slot, which], across,
        )

    def ywait(slot, which):
        here = part(block(yplane(slot), True), which)
        remote(here, here, ysend.at[slot, which], yrecv.at[slot, which], across).wait_recv()

    def mcopy(where, of_line, which, of_core, source=None):
        target = part(panel.at[where * 4 + 2 * of_line + of_core], which)
        slot = (where * 2 + of_line, which)
        return remote(
            target if source is None else part(source, which), target,
            msend.at[slot], mrecv.at[slot], mate,
        )

    def hand(where, of_partner, which, source=None):
        mcopy(where, 1 - line if of_partner else line, which, core, source).start()

    def from_mate(where, of_partner):
        for which in range(2):
            mcopy(where, 1 - line if of_partner else line, which, 1 - core).wait_recv()

    for which in range(2):
        for way in range(2):
            zcopy(False, 1, way, which).start()
        ycopy(0, which).start()
    own_copy = pltpu.make_async_copy(og_ref, panel.at[row], local_sem.at[0])
    own_copy.start()
    w_copy = pltpu.make_async_copy(w_ref, w_v, local_sem.at[1])
    w_copy.start()
    for which in range(2):
        hand(z, False, which, og_ref)

    act_copy.wait()
    acts[core, x, 2 * side + line] = acts_v[...].astype(F32).T.astype(BF16)

    def act_y(slot):
        mine = acts.at[core, x, 2 * side + line]
        return remote(mine, mine, aysend.at[slot], ayrecv.at[slot], (across, beside, corner)[slot])

    def act_y_wait(slot):
        place = (2 * side + 1 - line, 2 * (1 - side) + line, 2 * (1 - side) + 1 - line)[slot]
        here = acts.at[core, x, place]
        remote(here, here, aysend.at[slot], ayrecv.at[slot], across).wait_recv()

    def act_x(step):
        mine = acts.at[core, x]
        return remote(mine, mine, axsend.at[step], axrecv.at[step], x_peer(step))

    def act_x_wait(step):
        here = acts.at[core, lax.rem(x + 4 - step, 4)]
        remote(here, here, axsend.at[step], axrecv.at[step], x_peer(step)).wait_recv()

    def act_m(where, of_core):
        ref = acts.at[of_core, where]
        return remote(ref, ref, amsend.at[where], amrecv.at[where], mate)

    for slot in range(3):
        act_y(slot).start()

    def chunk(where, of_line, columns):
        return panel[pl.ds(where * 4 + 2 * of_line, 2), :, columns].reshape(64, columns.size)

    def wide_send(where, of_line):
        return remote(
            wide.at[where, of_line], wide_in.at[col, of_line],
            rsend.at[where, of_line], rrecv.at[col, of_line], (row, where),
        )

    def slim_send(where, of_line):
        return remote(
            slim.at[where, of_line], slim_in.at[col, of_line],
            rsend.at[where, of_line], rrecv.at[col, of_line], (row, where),
        )

    def input_grad(pieces):
        pieces = [(where, 1 - line if of_partner else line) for where, of_partner in pieces]

        def add(k, total):
            columns = pl.ds(pl.multiple_of(k * quarter, quarter), quarter)
            lhs = jnp.concatenate([chunk(*piece, columns) for piece in pieces], axis=0)
            return total + lax.dot_general(
                lhs, w_v[:, columns], (((1,), (1,)), ((), ())), preferred_element_type=F32
            )

        total = lax.fori_loop(0, 4, add, jnp.zeros((64 * len(pieces), w_v.shape[0]), F32))
        for i, (where, of_line) in enumerate(pieces):
            value = total[i * 64:(i + 1) * 64]
            same = lax.rem(where, 2) == side

            @pl.when(same)
            def _():
                wide[where, of_line] = value

            @pl.when(same & (where != col))
            def _():
                wide_send(where, of_line).start()

            @pl.when(jnp.logical_not(same))
            def _():
                slim[where, of_line] = value.astype(BF16)
                slim_send(where, of_line).start()

    def weight_grad(planes, first=False, last=False):
        def lhs_of(of_core, of_line):
            return jnp.concatenate(
                [acts[of_core, where // 2, 2 * lax.rem(where, 2) + of_line] for where in planes], axis=1
            )

        def rhs_of(columns):
            return jnp.concatenate(
                [panel[pl.ds(where * 4, 4), :, columns].reshape(128, columns.size) for where in planes],
                axis=0,
            )

        def own(t, carry):
            columns = pl.ds(pl.multiple_of(t * 512, 512), 512)
            out = jnp.dot(lhs_of(core, line), rhs_of(columns), preferred_element_type=F32)
            if not first:
                out = out + wacc[:, columns]
            if last:
                wg_ref[:, columns] = out.astype(BF16)
            else:
                wacc[:, columns] = out
            return carry

        lax.fori_loop(0, 8, own, 0)

        def others(t, carry):
            which = lax.rem(member + 1 + t // 2, 4)
            columns = pl.ds(pl.multiple_of(member * quarter + lax.rem(t, 2) * 512, 512), 512)
            place = pl.ds(pl.multiple_of(lax.rem(t, 2) * 512, 512), 512)
            out = jnp.dot(
                lhs_of(lax.rem(which, 2), which // 2), rhs_of(columns), preferred_element_type=F32
            )
            if not first:
                out = out + gacc[which, :, place]
            if last:
                g_ref[which, :, place] = out.astype(BF16)
            else:
                gacc[which, :, place] = out
            return carry

        lax.fori_loop(0, 6, others, 0)

    def pair(step):
        return [plane(step, 0), plane(step, 1)]

    def from_z(of_partner, step, which):
        for way in range(2):
            zwait(of_partner, step, way, which)
            if step < 3:
                zcopy(of_partner, step + 1, way, which).start()
            elif step == 3 and not of_partner and way == which:
                zcopy(False, 4, way, which).start()
            if step == 1:
                ycopy(1 + way, which).start()
            hand(plane(step, way), of_partner, which)

    def from_y_near(which):
        for way in range(2):
            ywait(1 + way, which)
            zcopy(True, 2, way, which).start()
            hand(plane(1, way), True, which)

    from_z(False, 1, 0)
    from_z(False, 1, 1)
    for which in range(2):
        ywait(0, which)
        hand(z, True, which)
    for slot in range(3):
        act_y_wait(slot)
    for step in range(1, 4):
        act_x(step).start()
    act_m(x, core).start()
    from_z(False, 2, 0)
    own_copy.wait()
    w_copy.wait()
    from_mate(z, False)
    from_z(False, 2, 1)
    from_y_near(0)
    from_mate(z, True)
    input_grad([(z, False), (z, True)])
    from_z(False, 3, 0)
    for where in pair(1):
        from_mate(where, False)
    input_grad([(where, False) for where in pair(1)])
    from_y_near(1)
    from_z(False, 3, 1)
    for step in range(1, 4):
        act_x_wait(step)
        act_m(lax.rem(x + 4 - step, 4), core).start()
    for where in pair(2):
        from_mate(where, False)
    input_grad([(where, False) for where in pair(2)])
    for way in range(2):
        zwait(False, 4, way, way)
        ycopy(3, way).start()
        hand(plane(4, 0), False, way)
    for where in pair(1):
        from_mate(where, True)
    input_grad([(where, True) for where in pair(1)])
    from_z(True, 2, 0)
    for where in pair(3):
        from_mate(where, False)
    input_grad([(where, False) for where in pair(3)])
    for where in range(4):
        act_m(where, 1 - core).wait_recv()
    from_z(True, 2, 1)
    weight_grad(pair(1), first=True)
    for which in range(2):
        ywait(3, which)
        hand(plane(4, 0), True, which)
    for where in pair(2):
        from_mate(where, True)
    input_grad([(where, True) for where in pair(2)])
    from_mate(plane(4, 0), False)
    from_mate(plane(4, 0), True)
    input_grad([(plane(4, 0), False), (plane(4, 0), True)])
    from_z(True, 3, 0)
    weight_grad(pair(2))
    weight_grad([z, plane(4, 0)])
    from_z(True, 3, 1)
    for where in pair(3):
        from_mate(where, True)
    input_grad([(where, True) for where in pair(3)])
    weight_grad(pair(3), last=True)
    g_ref[member] = wg_ref[:, pl.ds(pl.multiple_of(member * quarter, quarter), quarter)]

    for of_line in range(2):
        rows = pl.ds(of_line * 64, 64)

        def take_wide(step, total):
            where = lax.rem(x + step, 4) * 2 + side
            ref = wide_in.at[where, of_line]
            remote(ref, ref, rsend.at[where, of_line], rrecv.at[where, of_line], (row, where)).wait_recv()
            return total + wide_in[where, of_line]

        def take_slim(step, total):
            where = lax.rem(x + step, 4) * 2 + 1 - side
            ref = slim_in.at[where, of_line]
            remote(ref, ref, rsend.at[where, of_line], rrecv.at[where, of_line], (row, where)).wait_recv()
            return total + slim_in[where, of_line].astype(F32)

        total = lax.fori_loop(1, 4, take_wide, wide[col, of_line])
        ig_ref[rows, :] = lax.fori_loop(0, 4, take_slim, total).astype(BF16)

    for way in range(2):
        for which in range(2):
            for step in range(1, 4):
                zcopy(False, step, way, which).wait_send()
            for step in range(2, 4):
                zcopy(True, step, way, which).wait_send()
        zcopy(False, 4, way, way).wait_send()
    for slot in range(4):
        for which in range(2):
            ycopy(slot, which).wait_send()
    for slot in range(3):
        act_y(slot).wait_send()
        act_x(slot + 1).wait_send()

    def drain(where, carry):
        for of_line in range(2):
            for which in range(2):
                mcopy(where, of_line, which, core).wait_send()
        return carry

    lax.fori_loop(0, 8, drain, 0)
    for where in range(4):
        act_m(where, core).wait_send()

    def drain_sums(step, carry):
        for of_line in range(2):
            @pl.when(step > 0)
            def _():
                wide_send(lax.rem(x + step, 4) * 2 + side, of_line).wait_send()

            slim_send(lax.rem(x + step, 4) * 2 + 1 - side, of_line).wait_send()
        return carry

    lax.fori_loop(0, 4, drain_sums, 0)


def gram_kernel(g_ref, wg_in, left_ref, right_ref, wg_out):
    i = pl.program_id(0)
    size = left_ref.shape[0]
    rows = pl.ds(pl.multiple_of(i * size, size), size)
    wg_out[...] = wg_in[...]
    scale = 1.0 / g_ref.shape[0]
    left_ref[...] = scale * lax.dot_general(
        g_ref[rows, :], g_ref[...], (((1,), (1,)), ((), ())), preferred_element_type=F32
    )
    right_ref[...] = scale * lax.dot_general(
        g_ref[:, rows], g_ref[...], (((0,), (0,)), ((), ())), preferred_element_type=F32
    )


def on_device(activations, out_grad, weight):
    tokens, feats = activations.shape
    rows, cols = weight.shape
    vmem = pl.BlockSpec(memory_space=pltpu.VMEM)
    anywhere = pl.BlockSpec(memory_space=pltpu.HBM)
    dma = pltpu.SemaphoreType.DMA
    quarter = cols // 4
    input_grad, weight_grad, blocks = pl.pallas_call(
        gather_kernel,
        out_shape=(
            jax.ShapeDtypeStruct((tokens, feats), BF16),
            jax.ShapeDtypeStruct((rows, cols), BF16),
            jax.ShapeDtypeStruct((4, rows, quarter), BF16),
        ),
        in_specs=[anywhere, anywhere, anywhere],
        out_specs=(vmem, vmem, vmem),
        scratch_shapes=[
            pltpu.VMEM((32, out_grad.shape[0], cols), BF16),
            pltpu.VMEM((rows, cols), BF16),
            pltpu.VMEM((tokens, feats), BF16),
            pltpu.VMEM((2, 4, 4, feats, tokens), BF16),
            pltpu.VMEM((rows, cols), F32),
            pltpu.VMEM((4, rows, quarter), F32),
            pltpu.VMEM((8, 2, tokens // 2, feats), F32),
            pltpu.VMEM((8, 2, tokens // 2, feats), F32),
            pltpu.VMEM((8, 2, tokens // 2, feats), BF16),
            pltpu.VMEM((8, 2, tokens // 2, feats), BF16),
            dma((3,)),
            dma((2, 2, 4, 2)), dma((2, 2, 4, 2)), dma((4, 2)), dma((4, 2)), dma((16, 2)), dma((16, 2)),
            dma((3,)), dma((3,)), dma((4,)), dma((4,)), dma((4,)), dma((4,)), dma((8, 2)), dma((8, 2)),
        ],
        compiler_params=pltpu.CompilerParams(
            collective_id=0, has_side_effects=True, vmem_limit_bytes=44 * 2**20
        ),
        name="gather_and_grads",
    )(activations, out_grad, weight)

    size = 4 * rows
    step = size // 4
    left, right, weight_grad = pl.pallas_call(
        gram_kernel,
        grid=(4,),
        out_shape=(
            jax.ShapeDtypeStruct((size, quarter), F32),
            jax.ShapeDtypeStruct((quarter, quarter), F32),
            jax.ShapeDtypeStruct((rows, cols), BF16),
        ),
        in_specs=[
            pl.BlockSpec((size, quarter), lambda i: (0, 0)),
            pl.BlockSpec((rows // 4, cols), lambda i: (i, 0)),
        ],
        out_specs=(
            pl.BlockSpec((step, quarter), lambda i: (i, 0)),
            pl.BlockSpec((step, quarter), lambda i: (i, 0)),
            pl.BlockSpec((rows // 4, cols), lambda i: (i, 0)),
        ),
        compiler_params=pltpu.CompilerParams(vmem_limit_bytes=32 * 2**20),
        name="grams",
    )(blocks.reshape(size, quarter), weight_grad)
    return (
        input_grad,
        weight_grad,
        left.reshape(1, 1, 1, size, quarter),
        right.reshape(1, 1, 1, quarter, quarter),
    )


def solution(mesh):
    return jax.shard_map(
        on_device,
        mesh=mesh,
        in_specs=(P("col", "row"), P("row", "col"), P("row", "col")),
        out_specs=(
            P("col", "row"),
            P("row", "col"),
            P("row", "col", None, None, None),
            P("row", "col", None, None, None),
        ),
        check_vma=False,
    )
```

```python
import functools

import jax
import jax.numpy as jnp
from jax import lax
from jax.experimental import pallas as pl
from jax.experimental.pallas import tpu as pltpu
from jax.sharding import PartitionSpec as P

MESH = pl.DeviceIdType.MESH
F32 = jnp.float32
BF16 = jnp.bfloat16


def gather_kernel(
    acts_ref, og_ref, w_ref,
    ig_ref, wg_ref, g_ref,
    panel, w_v, acts_v, acts, wacc, gacc, wide, wide_in, slim, slim_in,
    local_sem, zsend, zrecv, ysend, yrecv, msend, mrecv,
    aysend, ayrecv, axsend, axrecv, amsend, amrecv, rsend, rrecv,
):
    row, col = lax.axis_index("row"), lax.axis_index("col")
    z, line, core = row // 4, lax.rem(row // 2, 2), lax.rem(row, 2)
    x, side = col // 2, lax.rem(col, 2)
    member = 2 * line + core
    half = og_ref.shape[0] // 2
    quarter = og_ref.shape[1] // 4
    up = (lax.rem(z + 1, 8) * 4 + member, col)
    down = (lax.rem(z + 7, 8) * 4 + member, col)
    far_row = z * 4 + 2 * (1 - line) + core
    across = (far_row, col)
    mate = (z * 4 + 2 * line + 1 - core, col)
    beside = (row, x * 2 + 1 - side)
    corner = (far_row, x * 2 + 1 - side)

    def x_peer(step, other=False):
        return (row, lax.rem(x + step, 4) * 2 + (1 - side if other else side))

    def remote(src, dst, send, recv, device):
        return pltpu.make_async_remote_copy(
            src_ref=src, dst_ref=dst, send_sem=send, recv_sem=recv,
            device_id=device, device_id_type=MESH,
        )

    act_copy = pltpu.make_async_copy(acts_ref, acts_v, local_sem.at[2])
    act_copy.start()
    barrier = pltpu.get_barrier_semaphore()
    peers = [up, down, across, mate, beside, corner]
    peers += [x_peer(step) for step in range(1, 4)] + [x_peer(step, True) for step in range(1, 4)]
    for device in peers:
        pl.semaphore_signal(barrier, inc=1, device_id=device, device_id_type=MESH)
    pl.semaphore_wait(barrier, len(peers))

    def plane(distance, way):
        return lax.rem(z + 8 - distance if way == 0 else z + distance, 8)

    def part(ref, which):
        return ref.at[pl.ds(which * half, half)]

    def block(where, of_partner):
        return panel.at[where * 4 + 2 * (1 - line if of_partner else line) + core]

    def zcopy(of_partner, step, way, which):
        slot = (way, int(of_partner), step - 1, which)
        target = block(plane(step - 1, way), of_partner)
        source = og_ref if step == 1 else target
        return remote(
            part(source, which), part(target, which),
            zsend.at[slot], zrecv.at[slot], up if way == 0 else down,
        )

    def zwait(of_partner, step, way, which):
        slot = (way, int(of_partner), step - 1, which)
        here = part(block(plane(step, way), of_partner), which)
        remote(here, here, zsend.at[slot], zrecv.at[slot], up if way == 0 else down).wait_recv()

    def yplane(slot):
        return (z, plane(1, 0), plane(1, 1), plane(4, 0))[slot]

    def ycopy(slot, which):
        target = block(yplane(slot), False)
        source = og_ref if slot == 0 else target
        return remote(
            part(source, which), part(target, which),
            ysend.at[slot, which], yrecv.at[slot, which], across,
        )

    def ywait(slot, which):
        here = part(block(yplane(slot), True), which)
        remote(here, here, ysend.at[slot, which], yrecv.at[slot, which], across).wait_recv()

    def mcopy(where, of_line, which, of_core, source=None):
        target = part(panel.at[where * 4 + 2 * of_line + of_core], which)
        slot = (where * 2 + of_line, which)
        return remote(
            target if source is None else part(source, which), target,
            msend.at[slot], mrecv.at[slot], mate,
        )

    def hand(where, of_partner, which, source=None):
        mcopy(where, 1 - line if of_partner else line, which, core, source).start()

    def from_mate(where, of_partner):
        for which in range(2):
            mcopy(where, 1 - line if of_partner else line, which, 1 - core).wait_recv()

    for which in range(2):
        for way in range(2):
            zcopy(False, 1, way, which).start()
        ycopy(0, which).start()
    own_copy = pltpu.make_async_copy(og_ref, panel.at[row], local_sem.at[0])
    own_copy.start()
    w_copy = pltpu.make_async_copy(w_ref, w_v, local_sem.at[1])
    w_copy.start()
    for which in range(2):
        hand(z, False, which, og_ref)

    act_copy.wait()
    acts[core, x, 2 * side + line] = acts_v[...].astype(F32).T.astype(BF16)

    def act_y(slot):
        mine = acts.at[core, x, 2 * side + line]
        return remote(mine, mine, aysend.at[slot], ayrecv.at[slot], (across, beside, corner)[slot])

    def act_y_wait(slot):
        place = (2 * side + 1 - line, 2 * (1 - side) + line, 2 * (1 - side) + 1 - line)[slot]
        here = acts.at[core, x, place]
        remote(here, here, aysend.at[slot], ayrecv.at[slot], across).wait_recv()

    def act_x(step):
        mine = acts.at[core, x]
        return remote(mine, mine, axsend.at[step], axrecv.at[step], x_peer(step))

    def act_x_wait(step):
        here = acts.at[core, lax.rem(x + 4 - step, 4)]
        remote(here, here, axsend.at[step], axrecv.at[step], x_peer(step)).wait_recv()

    def act_m(where, of_core):
        ref = acts.at[of_core, where]
        return remote(ref, ref, amsend.at[where], amrecv.at[where], mate)

    for slot in range(3):
        act_y(slot).start()

    def chunk(where, of_line, columns):
        return panel[pl.ds(where * 4 + 2 * of_line, 2), :, columns].reshape(64, columns.size)

    def wide_send(where, of_line):
        return remote(
            wide.at[where, of_line], wide_in.at[col, of_line],
            rsend.at[where, of_line], rrecv.at[col, of_line], (row, where),
        )

    def slim_send(where, of_line):
        return remote(
            slim.at[where, of_line], slim_in.at[col, of_line],
            rsend.at[where, of_line], rrecv.at[col, of_line], (row, where),
        )

    def input_grad(pieces):
        pieces = [(where, 1 - line if of_partner else line) for where, of_partner in pieces]

        lhs = jnp.concatenate([chunk(*piece, pl.ds(0, 4 * quarter)) for piece in pieces], axis=0)
        total = lax.dot_general(
            lhs, w_v[...], (((1,), (1,)), ((), ())), preferred_element_type=F32
        )
        for i, (where, of_line) in enumerate(pieces):
            value = total[i * 64:(i + 1) * 64]
            same = lax.rem(where, 2) == side

            @pl.when(same)
            def _():
                wide[where, of_line] = value

            @pl.when(same & (where != col))
            def _():
                wide_send(where, of_line).start()

            @pl.when(jnp.logical_not(same))
            def _():
                slim[where, of_line] = value.astype(BF16)
                slim_send(where, of_line).start()

    def weight_grad(planes, first=False, last=False):
        def lhs_of(of_core, of_line):
            return jnp.concatenate(
                [acts[of_core, where // 2, 2 * lax.rem(where, 2) + of_line] for where in planes], axis=1
            )

        def rhs_of(columns):
            return jnp.concatenate(
                [panel[pl.ds(where * 4, 4), :, columns].reshape(128, columns.size) for where in planes],
                axis=0,
            )

        def own(t, carry):
            columns = pl.ds(pl.multiple_of(t * quarter, quarter), quarter)
            out = jnp.dot(lhs_of(core, line), rhs_of(columns), preferred_element_type=F32)
            if not first:
                out = out + wacc[:, columns]
            if last:
                wg_ref[:, columns] = out.astype(BF16)
            else:
                wacc[:, columns] = out
            return carry

        lax.fori_loop(0, 4, own, 0)

        def others(t, carry):
            which = lax.rem(member + 1 + t, 4)
            columns = pl.ds(pl.multiple_of(member * quarter, quarter), quarter)
            out = jnp.dot(
                lhs_of(lax.rem(which, 2), which // 2), rhs_of(columns), preferred_element_type=F32
            )
            if not first:
                out = out + gacc[which]
            if last:
                g_ref[which] = out.astype(BF16)
            else:
                gacc[which] = out
            return carry

        lax.fori_loop(0, 3, others, 0)

    def pair(step):
        return [plane(step, 0), plane(step, 1)]

    def from_z(of_partner, step, which):
        for way in range(2):
            zwait(of_partner, step, way, which)
            if step < 3:
                zcopy(of_partner, step + 1, way, which).start()
            elif step == 3 and not of_partner and way == which:
                zcopy(False, 4, way, which).start()
            if step == 1:
                ycopy(1 + way, which).start()
            hand(plane(step, way), of_partner, which)

    def from_y_near(which):
        for way in range(2):
            ywait(1 + way, which)
            zcopy(True, 2, way, which).start()
            hand(plane(1, way), True, which)

    from_z(False, 1, 0)
    from_z(False, 1, 1)
    for which in range(2):
        ywait(0, which)
        hand(z, True, which)
    for slot in range(3):
        act_y_wait(slot)
    for step in range(1, 4):
        act_x(step).start()
    act_m(x, core).start()
    from_z(False, 2, 0)
    own_copy.wait()
    w_copy.wait()
    from_mate(z, False)
    from_z(False, 2, 1)
    from_y_near(0)
    from_mate(z, True)
    input_grad([(z, False), (z, True)])
    from_z(False, 3, 0)
    for where in pair(1):
        from_mate(where, False)
    input_grad([(where, False) for where in pair(1)])
    from_y_near(1)
    from_z(False, 3, 1)
    for where in pair(2):
        from_mate(where, False)
    input_grad([(where, False) for where in pair(2)])
    for way in range(2):
        zwait(False, 4, way, way)
        ycopy(3, way).start()
        hand(plane(4, 0), False, way)
    for where in pair(1):
        from_mate(where, True)
    input_grad([(where, True) for where in pair(1)])
    for step in range(1, 4):
        act_x_wait(step)
        act_m(lax.rem(x + 4 - step, 4), core).start()
    from_z(True, 2, 0)
    for where in pair(3):
        from_mate(where, False)
    input_grad([(where, False) for where in pair(3)])
    for where in range(4):
        act_m(where, 1 - core).wait_recv()
    weight_grad([z] + pair(1), first=True)
    from_z(True, 2, 1)
    for which in range(2):
        ywait(3, which)
        hand(plane(4, 0), True, which)
    for where in pair(2):
        from_mate(where, True)
    input_grad([(where, True) for where in pair(2)])
    from_mate(plane(4, 0), False)
    from_mate(plane(4, 0), True)
    input_grad([(plane(4, 0), False), (plane(4, 0), True)])
    from_z(True, 3, 0)
    weight_grad(pair(2) + [plane(4, 0)])
    from_z(True, 3, 1)
    for where in pair(3):
        from_mate(where, True)
    input_grad([(where, True) for where in pair(3)])
    weight_grad(pair(3), last=True)
    g_ref[member] = wg_ref[:, pl.ds(pl.multiple_of(member * quarter, quarter), quarter)]

    for of_line in range(2):
        rows = pl.ds(of_line * 64, 64)

        def take_wide(step, total):
            where = lax.rem(x + step, 4) * 2 + side
            ref = wide_in.at[where, of_line]
            remote(ref, ref, rsend.at[where, of_line], rrecv.at[where, of_line], (row, where)).wait_recv()
            return total + wide_in[where, of_line]

        def take_slim(step, total):
            where = lax.rem(x + step, 4) * 2 + 1 - side
            ref = slim_in.at[where, of_line]
            remote(ref, ref, rsend.at[where, of_line], rrecv.at[where, of_line], (row, where)).wait_recv()
            return total + slim_in[where, of_line].astype(F32)

        total = lax.fori_loop(1, 4, take_wide, wide[col, of_line])
        ig_ref[rows, :] = lax.fori_loop(0, 4, take_slim, total).astype(BF16)

    for way in range(2):
        for which in range(2):
            for step in range(1, 4):
                zcopy(False, step, way, which).wait_send()
            for step in range(2, 4):
                zcopy(True, step, way, which).wait_send()
        zcopy(False, 4, way, way).wait_send()
    for slot in range(4):
        for which in range(2):
            ycopy(slot, which).wait_send()
    for slot in range(3):
        act_y(slot).wait_send()
        act_x(slot + 1).wait_send()

    def drain(where, carry):
        for of_line in range(2):
            for which in range(2):
                mcopy(where, of_line, which, core).wait_send()
        return carry

    lax.fori_loop(0, 8, drain, 0)
    for where in range(4):
        act_m(where, core).wait_send()

    def drain_sums(step, carry):
        for of_line in range(2):
            @pl.when(step > 0)
            def _():
                wide_send(lax.rem(x + step, 4) * 2 + side, of_line).wait_send()

            slim_send(lax.rem(x + step, 4) * 2 + 1 - side, of_line).wait_send()
        return carry

    lax.fori_loop(0, 4, drain_sums, 0)


def gram_kernel(g_ref, wg_in, left_ref, right_ref, wg_out):
    i = pl.program_id(0)
    size = left_ref.shape[0]
    rows = pl.ds(pl.multiple_of(i * size, size), size)
    wg_out[...] = wg_in[...]
    scale = 1.0 / g_ref.shape[0]
    left_ref[...] = scale * lax.dot_general(
        g_ref[rows, :], g_ref[...], (((1,), (1,)), ((), ())), preferred_element_type=F32
    )
    right_ref[...] = scale * lax.dot_general(
        g_ref[:, rows], g_ref[...], (((0,), (0,)), ((), ())), preferred_element_type=F32
    )


def on_device(activations, out_grad, weight):
    tokens, feats = activations.shape
    rows, cols = weight.shape
    vmem = pl.BlockSpec(memory_space=pltpu.VMEM)
    anywhere = pl.BlockSpec(memory_space=pl.ANY)
    dma = pltpu.SemaphoreType.DMA
    quarter = cols // 4
    input_grad, weight_grad, blocks = pl.pallas_call(
        gather_kernel,
        out_shape=(
            jax.ShapeDtypeStruct((tokens, feats), BF16),
            jax.ShapeDtypeStruct((rows, cols), BF16),
            jax.ShapeDtypeStruct((4, rows, quarter), BF16),
        ),
        in_specs=[anywhere, anywhere, anywhere],
        out_specs=(vmem, vmem, vmem),
        scratch_shapes=[
            pltpu.VMEM((32, out_grad.shape[0], cols), BF16),
            pltpu.VMEM((rows, cols), BF16),
            pltpu.VMEM((tokens, feats), BF16),
            pltpu.VMEM((2, 4, 4, feats, tokens), BF16),
            pltpu.VMEM((rows, cols), F32),
            pltpu.VMEM((4, rows, quarter), F32),
            pltpu.VMEM((8, 2, tokens // 2, feats), F32),
            pltpu.VMEM((8, 2, tokens // 2, feats), F32),
            pltpu.VMEM((8, 2, tokens // 2, feats), BF16),
            pltpu.VMEM((8, 2, tokens // 2, feats), BF16),
            dma((3,)),
            dma((2, 2, 4, 2)), dma((2, 2, 4, 2)), dma((4, 2)), dma((4, 2)), dma((16, 2)), dma((16, 2)),
            dma((3,)), dma((3,)), dma((4,)), dma((4,)), dma((4,)), dma((4,)), dma((8, 2)), dma((8, 2)),
        ],
        compiler_params=pltpu.CompilerParams(
            collective_id=0, has_side_effects=True, vmem_limit_bytes=44 * 2**20
        ),
        name="gather_and_grads",
    )(*[pltpu.with_memory_space_constraint(a, pltpu.HBM) for a in (activations, out_grad, weight)])

    size = 4 * rows
    step = size // 4
    left, right, weight_grad = pl.pallas_call(
        gram_kernel,
        grid=(4,),
        out_shape=(
            jax.ShapeDtypeStruct((size, quarter), F32),
            jax.ShapeDtypeStruct((quarter, quarter), F32),
            jax.ShapeDtypeStruct((rows, cols), BF16),
        ),
        in_specs=[
            pl.BlockSpec((size, quarter), lambda i: (0, 0)),
            pl.BlockSpec((rows // 4, cols), lambda i: (i, 0)),
        ],
        out_specs=(
            pl.BlockSpec((step, quarter), lambda i: (i, 0)),
            pl.BlockSpec((step, quarter), lambda i: (i, 0)),
            pl.BlockSpec((rows // 4, cols), lambda i: (i, 0)),
        ),
        compiler_params=pltpu.CompilerParams(vmem_limit_bytes=32 * 2**20),
        name="grams",
    )(blocks.reshape(size, quarter), weight_grad)
    return (
        input_grad,
        weight_grad,
        left.reshape(1, 1, 1, size, quarter),
        right.reshape(1, 1, 1, quarter, quarter),
    )


def solution(mesh):
    return jax.shard_map(
        on_device,
        mesh=mesh,
        in_specs=(P("col", "row"), P("row", "col"), P("row", "col")),
        out_specs=(
            P("col", "row"),
            P("row", "col"),
            P("row", "col", None, None, None),
            P("row", "col", None, None, None),
        ),
        check_vma=False,
    )
```

```python
import functools

import jax
import jax.numpy as jnp
from jax import lax
from jax.experimental import pallas as pl
from jax.experimental.pallas import tpu as pltpu
from jax.sharding import PartitionSpec as P

MESH = pl.DeviceIdType.MESH
F32 = jnp.float32
BF16 = jnp.bfloat16


def gather_kernel(
    acts_ref, og_ref, w_ref,
    ig_ref, wg_ref, g_ref,
    panel, w_v, acts_v, acts, wide, wide_in, slim, slim_in,
    local_sem, zsend, zrecv, ysend, yrecv, msend, mrecv,
    aysend, ayrecv, axsend, axrecv, amsend, amrecv, rsend, rrecv,
):
    row, col = lax.axis_index("row"), lax.axis_index("col")
    z, line, core = row // 4, lax.rem(row // 2, 2), lax.rem(row, 2)
    x, side = col // 2, lax.rem(col, 2)
    member = 2 * line + core
    half = og_ref.shape[0] // 2
    quarter = og_ref.shape[1] // 4
    up = (lax.rem(z + 1, 8) * 4 + member, col)
    down = (lax.rem(z + 7, 8) * 4 + member, col)
    far_row = z * 4 + 2 * (1 - line) + core
    across = (far_row, col)
    mate = (z * 4 + 2 * line + 1 - core, col)
    beside = (row, x * 2 + 1 - side)
    corner = (far_row, x * 2 + 1 - side)

    def x_peer(step, other=False):
        return (row, lax.rem(x + step, 4) * 2 + (1 - side if other else side))

    def remote(src, dst, send, recv, device):
        return pltpu.make_async_remote_copy(
            src_ref=src, dst_ref=dst, send_sem=send, recv_sem=recv,
            device_id=device, device_id_type=MESH,
        )

    act_copy = pltpu.make_async_copy(acts_ref, acts_v, local_sem.at[2])
    act_copy.start()
    barrier = pltpu.get_barrier_semaphore()
    peers = [up, down, across, mate, beside, corner]
    peers += [x_peer(step) for step in range(1, 4)] + [x_peer(step, True) for step in range(1, 4)]
    for device in peers:
        pl.semaphore_signal(barrier, inc=1, device_id=device, device_id_type=MESH)
    pl.semaphore_wait(barrier, len(peers))

    def plane(distance, way):
        return lax.rem(z + 8 - distance if way == 0 else z + distance, 8)

    def part(ref, which):
        return ref.at[pl.ds(which * half, half)]

    def block(where, of_partner):
        return panel.at[where * 4 + 2 * (1 - line if of_partner else line) + core]

    def zcopy(of_partner, step, way, which):
        slot = (way, int(of_partner), step - 1, which)
        target = block(plane(step - 1, way), of_partner)
        source = og_ref if step == 1 else target
        return remote(
            part(source, which), part(target, which),
            zsend.at[slot], zrecv.at[slot], up if way == 0 else down,
        )

    def zwait(of_partner, step, way, which):
        slot = (way, int(of_partner), step - 1, which)
        here = part(block(plane(step, way), of_partner), which)
        remote(here, here, zsend.at[slot], zrecv.at[slot], up if way == 0 else down).wait_recv()

    def yplane(slot):
        return (z, plane(1, 0), plane(1, 1), plane(4, 0))[slot]

    def ycopy(slot, which):
        target = block(yplane(slot), False)
        source = og_ref if slot == 0 else target
        return remote(
            part(source, which), part(target, which),
            ysend.at[slot, which], yrecv.at[slot, which], across,
        )

    def ywait(slot, which):
        here = part(block(yplane(slot), True), which)
        remote(here, here, ysend.at[slot, which], yrecv.at[slot, which], across).wait_recv()

    def mcopy(where, of_line, which, of_core, source=None):
        target = part(panel.at[where * 4 + 2 * of_line + of_core], which)
        slot = (where * 2 + of_line, which)
        return remote(
            target if source is None else part(source, which), target,
            msend.at[slot], mrecv.at[slot], mate,
        )

    def hand(where, of_partner, which, source=None):
        mcopy(where, 1 - line if of_partner else line, which, core, source).start()

    def from_mate(where, of_partner):
        for which in range(2):
            mcopy(where, 1 - line if of_partner else line, which, 1 - core).wait_recv()

    for which in range(2):
        for way in range(2):
            zcopy(False, 1, way, which).start()
        ycopy(0, which).start()
    own_copy = pltpu.make_async_copy(og_ref, panel.at[row], local_sem.at[0])
    own_copy.start()
    w_copy = pltpu.make_async_copy(w_ref, w_v, local_sem.at[1])
    w_copy.start()
    for which in range(2):
        hand(z, False, which, og_ref)

    act_copy.wait()
    acts[core, x, 2 * side + line] = acts_v[...].astype(F32).T.astype(BF16)

    def act_y(slot):
        mine = acts.at[core, x, 2 * side + line]
        return remote(mine, mine, aysend.at[slot], ayrecv.at[slot], (across, beside, corner)[slot])

    def act_y_wait(slot):
        place = (2 * side + 1 - line, 2 * (1 - side) + line, 2 * (1 - side) + 1 - line)[slot]
        here = acts.at[core, x, place]
        remote(here, here, aysend.at[slot], ayrecv.at[slot], across).wait_recv()

    def act_x(step):
        mine = acts.at[core, x]
        return remote(mine, mine, axsend.at[step], axrecv.at[step], x_peer(step))

    def act_x_wait(step):
        here = acts.at[core, lax.rem(x + 4 - step, 4)]
        remote(here, here, axsend.at[step], axrecv.at[step], x_peer(step)).wait_recv()

    def act_m(where, of_core):
        ref = acts.at[of_core, where]
        return remote(ref, ref, amsend.at[where], amrecv.at[where], mate)

    for slot in range(3):
        act_y(slot).start()

    def chunk(where, of_line, columns):
        return panel[pl.ds(where * 4 + 2 * of_line, 2), :, columns].reshape(64, columns.size)

    def wide_send(where, of_line):
        return remote(
            wide.at[where, of_line], wide_in.at[col, of_line],
            rsend.at[where, of_line], rrecv.at[col, of_line], (row, where),
        )

    def slim_send(where, of_line):
        return remote(
            slim.at[where, of_line], slim_in.at[col, of_line],
            rsend.at[where, of_line], rrecv.at[col, of_line], (row, where),
        )

    def input_grad(pieces):
        pieces = [(where, 1 - line if of_partner else line) for where, of_partner in pieces]

        lhs = jnp.concatenate([chunk(*piece, pl.ds(0, 4 * quarter)) for piece in pieces], axis=0)
        total = lax.dot_general(
            lhs, w_v[...], (((1,), (1,)), ((), ())), preferred_element_type=F32
        )
        for i, (where, of_line) in enumerate(pieces):
            value = total[i * 64:(i + 1) * 64]
            same = lax.rem(where, 2) == side

            @pl.when(same)
            def _():
                wide[where, of_line] = value

            @pl.when(same & (where != col))
            def _():
                wide_send(where, of_line).start()

            @pl.when(jnp.logical_not(same))
            def _():
                slim[where, of_line] = value.astype(BF16)
                slim_send(where, of_line).start()

    def weight_grad(planes):
        def lhs_of(of_core, of_line):
            return jnp.concatenate(
                [acts[of_core, where // 2, 2 * lax.rem(where, 2) + of_line] for where in planes], axis=1
            )

        def rhs_of(columns):
            return jnp.concatenate(
                [panel[pl.ds(where * 4, 4), :, columns].reshape(128, columns.size) for where in planes],
                axis=0,
            )

        def own(t, carry):
            columns = pl.ds(pl.multiple_of(t * quarter, quarter), quarter)
            out = jnp.dot(lhs_of(core, line), rhs_of(columns), preferred_element_type=F32)
            wg_ref[:, columns] = out.astype(BF16)
            return carry

        lax.fori_loop(0, 4, own, 0)

        def others(t, carry):
            which = lax.rem(member + 1 + t, 4)
            columns = pl.ds(pl.multiple_of(member * quarter, quarter), quarter)
            out = jnp.dot(
                lhs_of(lax.rem(which, 2), which // 2), rhs_of(columns), preferred_element_type=F32
            )
            g_ref[which] = out.astype(BF16)
            return carry

        lax.fori_loop(0, 3, others, 0)

    def pair(step):
        return [plane(step, 0), plane(step, 1)]

    def from_z(of_partner, step, which):
        for way in range(2):
            zwait(of_partner, step, way, which)
            if step < 3:
                zcopy(of_partner, step + 1, way, which).start()
            elif step == 3 and not of_partner and way == which:
                zcopy(False, 4, way, which).start()
            if step == 1:
                ycopy(1 + way, which).start()
            hand(plane(step, way), of_partner, which)

    def from_y_near(which):
        for way in range(2):
            ywait(1 + way, which)
            zcopy(True, 2, way, which).start()
            hand(plane(1, way), True, which)

    from_z(False, 1, 0)
    from_z(False, 1, 1)
    for which in range(2):
        ywait(0, which)
        hand(z, True, which)
    for slot in range(3):
        act_y_wait(slot)
    for step in range(1, 4):
        act_x(step).start()
    act_m(x, core).start()
    from_z(False, 2, 0)
    own_copy.wait()
    w_copy.wait()
    from_mate(z, False)
    from_z(False, 2, 1)
    from_y_near(0)
    from_mate(z, True)
    input_grad([(z, False), (z, True)])
    from_z(False, 3, 0)
    for where in pair(1):
        from_mate(where, False)
    input_grad([(where, False) for where in pair(1)])
    from_y_near(1)
    from_z(False, 3, 1)
    for where in pair(2):
        from_mate(where, False)
    input_grad([(where, False) for where in pair(2)])
    for way in range(2):
        zwait(False, 4, way, way)
        ycopy(3, way).start()
        hand(plane(4, 0), False, way)
    for where in pair(1):
        from_mate(where, True)
    input_grad([(where, True) for where in pair(1)])
    for step in range(1, 4):
        act_x_wait(step)
        act_m(lax.rem(x + 4 - step, 4), core).start()
    from_z(True, 2, 0)
    for where in pair(3):
        from_mate(where, False)
    input_grad([(where, False) for where in pair(3)])
    from_z(True, 2, 1)
    for where in pair(2):
        from_mate(where, True)
    input_grad([(where, True) for where in pair(2)])
    for where in range(4):
        act_m(where, 1 - core).wait_recv()
    for which in range(2):
        ywait(3, which)
        hand(plane(4, 0), True, which)
    from_z(True, 3, 0)
    from_mate(plane(4, 0), False)
    from_mate(plane(4, 0), True)
    input_grad([(plane(4, 0), False), (plane(4, 0), True)])
    from_z(True, 3, 1)
    for where in pair(3):
        from_mate(where, True)
    input_grad([(where, True) for where in pair(3)])
    weight_grad([z] + pair(1) + pair(2) + pair(3) + [plane(4, 0)])
    g_ref[member] = wg_ref[:, pl.ds(pl.multiple_of(member * quarter, quarter), quarter)]

    for of_line in range(2):
        rows = pl.ds(of_line * 64, 64)

        def take_wide(step, total):
            where = lax.rem(x + step, 4) * 2 + side
            ref = wide_in.at[where, of_line]
            remote(ref, ref, rsend.at[where, of_line], rrecv.at[where, of_line], (row, where)).wait_recv()
            return total + wide_in[where, of_line]

        def take_slim(step, total):
            where = lax.rem(x + step, 4) * 2 + 1 - side
            ref = slim_in.at[where, of_line]
            remote(ref, ref, rsend.at[where, of_line], rrecv.at[where, of_line], (row, where)).wait_recv()
            return total + slim_in[where, of_line].astype(F32)

        total = lax.fori_loop(1, 4, take_wide, wide[col, of_line])
        ig_ref[rows, :] = lax.fori_loop(0, 4, take_slim, total).astype(BF16)

    for way in range(2):
        for which in range(2):
            for step in range(1, 4):
                zcopy(False, step, way, which).wait_send()
            for step in range(2, 4):
                zcopy(True, step, way, which).wait_send()
        zcopy(False, 4, way, way).wait_send()
    for slot in range(4):
        for which in range(2):
            ycopy(slot, which).wait_send()
    for slot in range(3):
        act_y(slot).wait_send()
        act_x(slot + 1).wait_send()

    def drain(where, carry):
        for of_line in range(2):
            for which in range(2):
                mcopy(where, of_line, which, core).wait_send()
        return carry

    lax.fori_loop(0, 8, drain, 0)
    for where in range(4):
        act_m(where, core).wait_send()

    def drain_sums(step, carry):
        for of_line in range(2):
            @pl.when(step > 0)
            def _():
                wide_send(lax.rem(x + step, 4) * 2 + side, of_line).wait_send()

            slim_send(lax.rem(x + step, 4) * 2 + 1 - side, of_line).wait_send()
        return carry

    lax.fori_loop(0, 4, drain_sums, 0)


def gram_kernel(g_ref, wg_in, left_ref, right_ref, wg_out, left_v, right_v, sem):
    size = g_ref.shape[0]
    step = size // 4
    scale = 1.0 / size
    copies = [pltpu.make_async_copy(wg_in, wg_out, sem.at[8])]
    copies[0].start()
    for kind, (out_v, out_ref) in enumerate(((left_v, left_ref), (right_v, right_ref))):
        for i in range(4):
            low = i * step
            if kind == 0:
                out = lax.dot_general(
                    g_ref[low:low + step, :], g_ref[low:, :], (((1,), (1,)), ((), ())),
                    preferred_element_type=F32,
                )
            else:
                out = lax.dot_general(
                    g_ref[:, low:low + step], g_ref[:, low:], (((0,), (0,)), ((), ())),
                    preferred_element_type=F32,
                )
            out = out * scale
            out_v[low:low + step, low:] = out
            for j in range(i + 1, 4):
                block = out[:, (j - i) * step:(j - i + 1) * step]
                out_v[j * step:(j + 1) * step, low:low + step] = block.T
            rows = pl.ds(low, step)
            copy = pltpu.make_async_copy(out_v.at[rows], out_ref.at[rows], sem.at[kind * 4 + i])
            copy.start()
            copies.append(copy)
    for copy in copies:
        copy.wait()


def on_device(activations, out_grad, weight):
    tokens, feats = activations.shape
    rows, cols = weight.shape
    vmem = pl.BlockSpec(memory_space=pltpu.VMEM)
    anywhere = pl.BlockSpec(memory_space=pl.ANY)
    dma = pltpu.SemaphoreType.DMA
    quarter = cols // 4
    input_grad, weight_grad, blocks = pl.pallas_call(
        gather_kernel,
        out_shape=(
            jax.ShapeDtypeStruct((tokens, feats), BF16),
            jax.ShapeDtypeStruct((rows, cols), BF16),
            jax.ShapeDtypeStruct((4, rows, quarter), BF16),
        ),
        in_specs=[anywhere, anywhere, anywhere],
        out_specs=(vmem, vmem, vmem),
        scratch_shapes=[
            pltpu.VMEM((32, out_grad.shape[0], cols), BF16),
            pltpu.VMEM((rows, cols), BF16),
            pltpu.VMEM((tokens, feats), BF16),
            pltpu.VMEM((2, 4, 4, feats, tokens), BF16),
            pltpu.VMEM((8, 2, tokens // 2, feats), F32),
            pltpu.VMEM((8, 2, tokens // 2, feats), F32),
            pltpu.VMEM((8, 2, tokens // 2, feats), BF16),
            pltpu.VMEM((8, 2, tokens // 2, feats), BF16),
            dma((3,)),
            dma((2, 2, 4, 2)), dma((2, 2, 4, 2)), dma((4, 2)), dma((4, 2)), dma((16, 2)), dma((16, 2)),
            dma((3,)), dma((3,)), dma((4,)), dma((4,)), dma((4,)), dma((4,)), dma((8, 2)), dma((8, 2)),
        ],
        compiler_params=pltpu.CompilerParams(
            collective_id=0, has_side_effects=True, vmem_limit_bytes=44 * 2**20
        ),
        name="gather_and_grads",
    )(*[pltpu.with_memory_space_constraint(a, pltpu.HBM) for a in (activations, out_grad, weight)])

    size = 4 * rows
    left, right, weight_grad = pl.pallas_call(
        gram_kernel,
        out_shape=(
            jax.ShapeDtypeStruct((size, quarter), F32),
            jax.ShapeDtypeStruct((quarter, quarter), F32),
            jax.ShapeDtypeStruct((rows, cols), BF16),
        ),
        in_specs=[vmem, vmem],
        out_specs=(anywhere, anywhere, anywhere),
        scratch_shapes=[
            pltpu.VMEM((size, quarter), F32), pltpu.VMEM((quarter, quarter), F32), dma((9,)),
        ],
        compiler_params=pltpu.CompilerParams(vmem_limit_bytes=32 * 2**20),
        name="grams",
    )(blocks.reshape(size, quarter), weight_grad)
    return (
        input_grad,
        weight_grad,
        left.reshape(1, 1, 1, size, quarter),
        right.reshape(1, 1, 1, quarter, quarter),
    )


def solution(mesh):
    return jax.shard_map(
        on_device,
        mesh=mesh,
        in_specs=(P("col", "row"), P("row", "col"), P("row", "col")),
        out_specs=(
            P("col", "row"),
            P("row", "col"),
            P("row", "col", None, None, None),
            P("row", "col", None, None, None),
        ),
        check_vma=False,
    )
```

```python
import functools

import jax
import jax.numpy as jnp
from jax import lax
from jax.experimental import pallas as pl
from jax.experimental.pallas import tpu as pltpu
from jax.sharding import PartitionSpec as P

MESH = pl.DeviceIdType.MESH
F32 = jnp.float32
BF16 = jnp.bfloat16


def gather_kernel(
    acts_ref, og_ref, w_ref,
    ig_ref, wg_ref, g_ref,
    panel, w_v, acts_v, acts, wide, wide_in, slim, slim_in,
    local_sem, zsend, zrecv, ysend, yrecv, msend, mrecv,
    aysend, ayrecv, axsend, axrecv, amsend, amrecv, rsend, rrecv,
):
    row, col = lax.axis_index("row"), lax.axis_index("col")
    z, line, core = row // 4, lax.rem(row // 2, 2), lax.rem(row, 2)
    x, side = col // 2, lax.rem(col, 2)
    member = 2 * line + core
    half = og_ref.shape[0] // 2
    quarter = og_ref.shape[1] // 4
    up = (lax.rem(z + 1, 8) * 4 + member, col)
    down = (lax.rem(z + 7, 8) * 4 + member, col)
    far_row = z * 4 + 2 * (1 - line) + core
    across = (far_row, col)
    mate = (z * 4 + 2 * line + 1 - core, col)
    beside = (row, x * 2 + 1 - side)
    corner = (far_row, x * 2 + 1 - side)

    def x_peer(step, other=False):
        return (row, lax.rem(x + step, 4) * 2 + (1 - side if other else side))

    def remote(src, dst, send, recv, device):
        return pltpu.make_async_remote_copy(
            src_ref=src, dst_ref=dst, send_sem=send, recv_sem=recv,
            device_id=device, device_id_type=MESH,
        )

    act_copy = pltpu.make_async_copy(acts_ref, acts_v, local_sem.at[2])
    act_copy.start()
    barrier = pltpu.get_barrier_semaphore()
    peers = [up, down, across, mate, beside, corner]
    peers += [x_peer(step) for step in range(1, 4)] + [x_peer(step, True) for step in range(1, 4)]
    for device in peers:
        pl.semaphore_signal(barrier, inc=1, device_id=device, device_id_type=MESH)
    pl.semaphore_wait(barrier, len(peers))

    def plane(distance, way):
        return lax.rem(z + 8 - distance if way == 0 else z + distance, 8)

    def part(ref, which):
        return ref.at[pl.ds(which * half, half)]

    def block(where, of_partner):
        return panel.at[where * 4 + 2 * (1 - line if of_partner else line) + core]

    def zcopy(of_partner, step, way, which):
        slot = (way, int(of_partner), step - 1, which)
        target = block(plane(step - 1, way), of_partner)
        source = og_ref if step == 1 else target
        return remote(
            part(source, which), part(target, which),
            zsend.at[slot], zrecv.at[slot], up if way == 0 else down,
        )

    def zwait(of_partner, step, way, which):
        slot = (way, int(of_partner), step - 1, which)
        here = part(block(plane(step, way), of_partner), which)
        remote(here, here, zsend.at[slot], zrecv.at[slot], up if way == 0 else down).wait_recv()

    def yplane(slot):
        return (z, plane(1, 0), plane(1, 1), plane(4, 0))[slot]

    def ycopy(slot, which):
        target = block(yplane(slot), False)
        source = og_ref if slot == 0 else target
        return remote(
            part(source, which), part(target, which),
            ysend.at[slot, which], yrecv.at[slot, which], across,
        )

    def ywait(slot, which):
        here = part(block(yplane(slot), True), which)
        remote(here, here, ysend.at[slot, which], yrecv.at[slot, which], across).wait_recv()

    def mcopy(where, of_line, which, of_core, source=None):
        target = part(panel.at[where * 4 + 2 * of_line + of_core], which)
        slot = (where * 2 + of_line, which)
        return remote(
            target if source is None else part(source, which), target,
            msend.at[slot], mrecv.at[slot], mate,
        )

    def hand(where, of_partner, which, source=None):
        mcopy(where, 1 - line if of_partner else line, which, core, source).start()

    def from_mate(where, of_partner):
        for which in range(2):
            mcopy(where, 1 - line if of_partner else line, which, 1 - core).wait_recv()

    for which in range(2):
        for way in range(2):
            zcopy(False, 1, way, which).start()
        ycopy(0, which).start()
    own_copy = pltpu.make_async_copy(og_ref, panel.at[row], local_sem.at[0])
    own_copy.start()
    w_copy = pltpu.make_async_copy(w_ref, w_v, local_sem.at[1])
    w_copy.start()
    for which in range(2):
        hand(z, False, which, og_ref)

    act_copy.wait()
    acts[core, x, 2 * side + line] = acts_v[...].astype(F32).T.astype(BF16)

    def act_y(slot):
        mine = acts.at[core, x, 2 * side + line]
        return remote(mine, mine, aysend.at[slot], ayrecv.at[slot], (across, beside, corner)[slot])

    def act_y_wait(slot):
        place = (2 * side + 1 - line, 2 * (1 - side) + line, 2 * (1 - side) + 1 - line)[slot]
        here = acts.at[core, x, place]
        remote(here, here, aysend.at[slot], ayrecv.at[slot], across).wait_recv()

    def act_x(step):
        mine = acts.at[core, x]
        return remote(mine, mine, axsend.at[step], axrecv.at[step], x_peer(step))

    def act_x_wait(step):
        here = acts.at[core, lax.rem(x + 4 - step, 4)]
        remote(here, here, axsend.at[step], axrecv.at[step], x_peer(step)).wait_recv()

    def act_m(where, of_core):
        ref = acts.at[of_core, where]
        return remote(ref, ref, amsend.at[where], amrecv.at[where], mate)

    for slot in range(3):
        act_y(slot).start()

    def chunk(where, of_line, columns):
        return panel[pl.ds(where * 4 + 2 * of_line, 2), :, columns].reshape(64, columns.size)

    def wide_send(where, of_line):
        return remote(
            wide.at[where, of_line], wide_in.at[col, of_line],
            rsend.at[where, of_line], rrecv.at[col, of_line], (row, where),
        )

    def slim_send(where, of_line):
        return remote(
            slim.at[where, of_line], slim_in.at[col, of_line],
            rsend.at[where, of_line], rrecv.at[col, of_line], (row, where),
        )

    def input_grad(pieces):
        pieces = [(where, 1 - line if of_partner else line) for where, of_partner in pieces]

        lhs = jnp.concatenate([chunk(*piece, pl.ds(0, 4 * quarter)) for piece in pieces], axis=0)
        total = lax.dot_general(
            lhs, w_v[...], (((1,), (1,)), ((), ())), preferred_element_type=F32
        )
        for i, (where, of_line) in enumerate(pieces):
            value = total[i * 64:(i + 1) * 64]
            same = lax.rem(where, 2) == side

            @pl.when(same)
            def _():
                wide[where, of_line] = value

            @pl.when(same & (where != col))
            def _():
                wide_send(where, of_line).start()

            @pl.when(jnp.logical_not(same))
            def _():
                slim[where, of_line] = value.astype(BF16)
                slim_send(where, of_line).start()

    def weight_grad(planes):
        def lhs_of(of_core, of_line):
            return jnp.concatenate(
                [acts[of_core, where // 2, 2 * lax.rem(where, 2) + of_line] for where in planes], axis=1
            )

        def rhs_of(columns):
            return jnp.concatenate(
                [panel[pl.ds(where * 4, 4), :, columns].reshape(128, columns.size) for where in planes],
                axis=0,
            )

        def own(t, carry):
            columns = pl.ds(pl.multiple_of(t * quarter, quarter), quarter)
            out = jnp.dot(lhs_of(core, line), rhs_of(columns), preferred_element_type=F32)
            wg_ref[:, columns] = out.astype(BF16)
            return carry

        lax.fori_loop(0, 4, own, 0)

        def others(t, carry):
            which = lax.rem(member + 1 + t, 4)
            columns = pl.ds(pl.multiple_of(member * quarter, quarter), quarter)
            out = jnp.dot(
                lhs_of(lax.rem(which, 2), which // 2), rhs_of(columns), preferred_element_type=F32
            )
            g_ref[which] = out.astype(BF16)
            return carry

        lax.fori_loop(0, 3, others, 0)

    def pair(step):
        return [plane(step, 0), plane(step, 1)]

    def from_z(of_partner, step, which):
        for way in range(2):
            zwait(of_partner, step, way, which)
            if step < 3:
                zcopy(of_partner, step + 1, way, which).start()
            elif step == 3 and not of_partner and way == which:
                zcopy(False, 4, way, which).start()
            if step == 1:
                ycopy(1 + way, which).start()
            hand(plane(step, way), of_partner, which)

    def from_y_near(which):
        for way in range(2):
            ywait(1 + way, which)
            zcopy(True, 2, way, which).start()
            hand(plane(1, way), True, which)

    from_z(False, 1, 0)
    from_z(False, 1, 1)
    for which in range(2):
        ywait(0, which)
        hand(z, True, which)
    for slot in range(3):
        act_y_wait(slot)
    for step in range(1, 4):
        act_x(step).start()
    act_m(x, core).start()
    from_z(False, 2, 0)
    own_copy.wait()
    w_copy.wait()
    from_mate(z, False)
    from_z(False, 2, 1)
    from_mate(z, True)
    input_grad([(z, False), (z, True)])
    from_z(False, 3, 0)
    from_y_near(0)
    for where in pair(1):
        from_mate(where, False)
    input_grad([(where, False) for where in pair(1)])
    from_z(False, 3, 1)
    from_y_near(1)
    for where in pair(2):
        from_mate(where, False)
    input_grad([(where, False) for where in pair(2)])
    for way in range(2):
        zwait(False, 4, way, way)
        ycopy(3, way).start()
        hand(plane(4, 0), False, way)
    for where in pair(1):
        from_mate(where, True)
    input_grad([(where, True) for where in pair(1)])
    for step in range(1, 4):
        act_x_wait(step)
        act_m(lax.rem(x + 4 - step, 4), core).start()
    from_z(True, 2, 0)
    for where in pair(3):
        from_mate(where, False)
    from_mate(plane(4, 0), False)
    input_grad([(where, False) for where in pair(3)] + [(plane(4, 0), False)])
    from_z(True, 2, 1)
    for where in pair(2):
        from_mate(where, True)
    input_grad([(where, True) for where in pair(2)])
    for where in range(4):
        act_m(where, 1 - core).wait_recv()
    for which in range(2):
        ywait(3, which)
        hand(plane(4, 0), True, which)
    from_z(True, 3, 0)
    from_z(True, 3, 1)
    for where in pair(3):
        from_mate(where, True)
    from_mate(plane(4, 0), True)
    input_grad([(where, True) for where in pair(3)] + [(plane(4, 0), True)])
    weight_grad([z] + pair(1) + pair(2) + pair(3) + [plane(4, 0)])
    g_ref[member] = wg_ref[:, pl.ds(pl.multiple_of(member * quarter, quarter), quarter)]

    for of_line in range(2):
        rows = pl.ds(of_line * 64, 64)

        def take_wide(step, total):
            where = lax.rem(x + step, 4) * 2 + side
            ref = wide_in.at[where, of_line]
            remote(ref, ref, rsend.at[where, of_line], rrecv.at[where, of_line], (row, where)).wait_recv()
            return total + wide_in[where, of_line]

        def take_slim(step, total):
            where = lax.rem(x + step, 4) * 2 + 1 - side
            ref = slim_in.at[where, of_line]
            remote(ref, ref, rsend.at[where, of_line], rrecv.at[where, of_line], (row, where)).wait_recv()
            return total + slim_in[where, of_line].astype(F32)

        total = lax.fori_loop(1, 4, take_wide, wide[col, of_line])
        ig_ref[rows, :] = lax.fori_loop(0, 4, take_slim, total).astype(BF16)

    for way in range(2):
        for which in range(2):
            for step in range(1, 4):
                zcopy(False, step, way, which).wait_send()
            for step in range(2, 4):
                zcopy(True, step, way, which).wait_send()
        zcopy(False, 4, way, way).wait_send()
    for slot in range(4):
        for which in range(2):
            ycopy(slot, which).wait_send()
    for slot in range(3):
        act_y(slot).wait_send()
        act_x(slot + 1).wait_send()

    def drain(where, carry):
        for of_line in range(2):
            for which in range(2):
                mcopy(where, of_line, which, core).wait_send()
        return carry

    lax.fori_loop(0, 8, drain, 0)
    for where in range(4):
        act_m(where, core).wait_send()

    def drain_sums(step, carry):
        for of_line in range(2):
            @pl.when(step > 0)
            def _():
                wide_send(lax.rem(x + step, 4) * 2 + side, of_line).wait_send()

            slim_send(lax.rem(x + step, 4) * 2 + 1 - side, of_line).wait_send()
        return carry

    lax.fori_loop(0, 4, drain_sums, 0)


def gram_kernel(
    g_ref, wg_in, ig_in, left_ref, right_ref, wg_out, ig_out, left_v, right_v, sem
):
    size = g_ref.shape[0]
    step = size // 4
    scale = 1.0 / size
    copies = [
        pltpu.make_async_copy(wg_in, wg_out, sem.at[8]),
        pltpu.make_async_copy(ig_in, ig_out, sem.at[9]),
    ]
    for copy in copies:
        copy.start()
    for kind, (out_v, out_ref) in enumerate(((left_v, left_ref), (right_v, right_ref))):
        for i in range(4):
            low = i * step
            if kind == 0:
                out = lax.dot_general(
                    g_ref[low:low + step, :], g_ref[low:, :], (((1,), (1,)), ((), ())),
                    preferred_element_type=F32,
                )
            else:
                out = lax.dot_general(
                    g_ref[:, low:low + step], g_ref[:, low:], (((0,), (0,)), ((), ())),
                    preferred_element_type=F32,
                )
            out = out * scale
            out_v[low:low + step, low:] = out
            for j in range(i + 1, 4):
                block = out[:, (j - i) * step:(j - i + 1) * step]
                out_v[j * step:(j + 1) * step, low:low + step] = block.T
            rows = pl.ds(low, step)
            copy = pltpu.make_async_copy(out_v.at[rows], out_ref.at[rows], sem.at[kind * 4 + i])
            copy.start()
            copies.append(copy)
    for copy in copies:
        copy.wait()


def on_device(activations, out_grad, weight):
    tokens, feats = activations.shape
    rows, cols = weight.shape
    vmem = pl.BlockSpec(memory_space=pltpu.VMEM)
    anywhere = pl.BlockSpec(memory_space=pl.ANY)
    dma = pltpu.SemaphoreType.DMA
    quarter = cols // 4
    input_grad, weight_grad, blocks = pl.pallas_call(
        gather_kernel,
        out_shape=(
            jax.ShapeDtypeStruct((tokens, feats), BF16),
            jax.ShapeDtypeStruct((rows, cols), BF16),
            jax.ShapeDtypeStruct((4, rows, quarter), BF16),
        ),
        in_specs=[anywhere, anywhere, anywhere],
        out_specs=(vmem, vmem, vmem),
        scratch_shapes=[
            pltpu.VMEM((32, out_grad.shape[0], cols), BF16),
            pltpu.VMEM((rows, cols), BF16),
            pltpu.VMEM((tokens, feats), BF16),
            pltpu.VMEM((2, 4, 4, feats, tokens), BF16),
            pltpu.VMEM((8, 2, tokens // 2, feats), F32),
            pltpu.VMEM((8, 2, tokens // 2, feats), F32),
            pltpu.VMEM((8, 2, tokens // 2, feats), BF16),
            pltpu.VMEM((8, 2, tokens // 2, feats), BF16),
            dma((3,)),
            dma((2, 2, 4, 2)), dma((2, 2, 4, 2)), dma((4, 2)), dma((4, 2)), dma((16, 2)), dma((16, 2)),
            dma((3,)), dma((3,)), dma((4,)), dma((4,)), dma((4,)), dma((4,)), dma((8, 2)), dma((8, 2)),
        ],
        compiler_params=pltpu.CompilerParams(
            collective_id=0, has_side_effects=True, vmem_limit_bytes=44 * 2**20
        ),
        name="gather_and_grads",
    )(*[pltpu.with_memory_space_constraint(a, pltpu.HBM) for a in (activations, out_grad, weight)])

    size = 4 * rows
    left, right, weight_grad, input_grad = pl.pallas_call(
        gram_kernel,
        out_shape=(
            jax.ShapeDtypeStruct((size, quarter), F32),
            jax.ShapeDtypeStruct((quarter, quarter), F32),
            jax.ShapeDtypeStruct((rows, cols), BF16),
            jax.ShapeDtypeStruct((tokens, feats), BF16),
        ),
        in_specs=[vmem, vmem, vmem],
        out_specs=(anywhere,) * 4,
        scratch_shapes=[
            pltpu.VMEM((size, quarter), F32), pltpu.VMEM((quarter, quarter), F32), dma((10,)),
        ],
        compiler_params=pltpu.CompilerParams(vmem_limit_bytes=32 * 2**20),
        name="grams",
    )(blocks.reshape(size, quarter), weight_grad, input_grad)
    return (
        input_grad,
        weight_grad,
        left.reshape(1, 1, 1, size, quarter),
        right.reshape(1, 1, 1, quarter, quarter),
    )


def solution(mesh):
    return jax.shard_map(
        on_device,
        mesh=mesh,
        in_specs=(P("col", "row"), P("row", "col"), P("row", "col")),
        out_specs=(
            P("col", "row"),
            P("row", "col"),
            P("row", "col", None, None, None),
            P("row", "col", None, None, None),
        ),
        check_vma=False,
    )
```

```python
import functools

import jax
import jax.numpy as jnp
from jax import lax
from jax.experimental import pallas as pl
from jax.experimental.pallas import tpu as pltpu
from jax.sharding import PartitionSpec as P

MESH = pl.DeviceIdType.MESH
F32 = jnp.float32
BF16 = jnp.bfloat16


def gather_kernel(
    acts_ref, og_ref, w_ref,
    ig_ref, wg_ref, g_ref,
    panel, w_v, acts_v, acts, wide, wide_in, slim, slim_in,
    local_sem, zsend, zrecv, ysend, yrecv, msend, mrecv,
    aysend, ayrecv, axsend, axrecv, amsend, amrecv, rsend, rrecv,
):
    row, col = lax.axis_index("row"), lax.axis_index("col")
    z, line, core = row // 4, lax.rem(row // 2, 2), lax.rem(row, 2)
    x, side = col // 2, lax.rem(col, 2)
    member = 2 * line + core
    half = og_ref.shape[0] // 2
    quarter = og_ref.shape[1] // 4
    up = (lax.rem(z + 1, 8) * 4 + member, col)
    down = (lax.rem(z + 7, 8) * 4 + member, col)
    far_row = z * 4 + 2 * (1 - line) + core
    across = (far_row, col)
    mate = (z * 4 + 2 * line + 1 - core, col)
    beside = (row, x * 2 + 1 - side)
    corner = (far_row, x * 2 + 1 - side)

    def x_peer(step, other=False):
        return (row, lax.rem(x + step, 4) * 2 + (1 - side if other else side))

    def remote(src, dst, send, recv, device):
        return pltpu.make_async_remote_copy(
            src_ref=src, dst_ref=dst, send_sem=send, recv_sem=recv,
            device_id=device, device_id_type=MESH,
        )

    act_copy = pltpu.make_async_copy(acts_ref, acts_v, local_sem.at[2])
    act_copy.start()
    barrier = pltpu.get_barrier_semaphore()
    peers = [up, down, across, mate, beside, corner]
    peers += [x_peer(step) for step in range(1, 4)] + [x_peer(step, True) for step in range(1, 4)]
    for device in peers:
        pl.semaphore_signal(barrier, inc=1, device_id=device, device_id_type=MESH)
    pl.semaphore_wait(barrier, len(peers))

    def plane(distance, way):
        return lax.rem(z + 8 - distance if way == 0 else z + distance, 8)

    def part(ref, which):
        return ref.at[pl.ds(which * half, half)]

    def block(where, of_partner):
        return panel.at[where * 4 + 2 * (1 - line if of_partner else line) + core]

    def zcopy(of_partner, step, way, which):
        slot = (way, int(of_partner), step - 1, which)
        target = block(plane(step - 1, way), of_partner)
        source = og_ref if step == 1 else target
        return remote(
            part(source, which), part(target, which),
            zsend.at[slot], zrecv.at[slot], up if way == 0 else down,
        )

    def zwait(of_partner, step, way, which):
        slot = (way, int(of_partner), step - 1, which)
        here = part(block(plane(step, way), of_partner), which)
        remote(here, here, zsend.at[slot], zrecv.at[slot], up if way == 0 else down).wait_recv()

    def yplane(slot):
        return (z, plane(1, 0), plane(1, 1), plane(4, 0))[slot]

    def ycopy(slot, which):
        target = block(yplane(slot), False)
        source = og_ref if slot == 0 else target
        return remote(
            part(source, which), part(target, which),
            ysend.at[slot, which], yrecv.at[slot, which], across,
        )

    def ywait(slot, which):
        here = part(block(yplane(slot), True), which)
        remote(here, here, ysend.at[slot, which], yrecv.at[slot, which], across).wait_recv()

    def mcopy(where, of_line, which, of_core, source=None):
        target = part(panel.at[where * 4 + 2 * of_line + of_core], which)
        slot = (where * 2 + of_line, which)
        return remote(
            target if source is None else part(source, which), target,
            msend.at[slot], mrecv.at[slot], mate,
        )

    def hand(where, of_partner, which, source=None):
        mcopy(where, 1 - line if of_partner else line, which, core, source).start()

    def from_mate(where, of_partner):
        for which in range(2):
            mcopy(where, 1 - line if of_partner else line, which, 1 - core).wait_recv()

    for which in range(2):
        for way in range(2):
            zcopy(False, 1, way, which).start()
        ycopy(0, which).start()
    own_copy = pltpu.make_async_copy(og_ref, panel.at[row], local_sem.at[0])
    own_copy.start()
    w_copy = pltpu.make_async_copy(w_ref, w_v, local_sem.at[1])
    w_copy.start()
    for which in range(2):
        hand(z, False, which, og_ref)

    act_copy.wait()
    acts[core, x, 2 * side + line] = acts_v[...].astype(F32).T.astype(BF16)

    def act_y(slot):
        mine = acts.at[core, x, 2 * side + line]
        return remote(mine, mine, aysend.at[slot], ayrecv.at[slot], (across, beside, corner)[slot])

    def act_y_wait(slot):
        place = (2 * side + 1 - line, 2 * (1 - side) + line, 2 * (1 - side) + 1 - line)[slot]
        here = acts.at[core, x, place]
        remote(here, here, aysend.at[slot], ayrecv.at[slot], across).wait_recv()

    def act_x(step):
        mine = acts.at[core, x]
        return remote(mine, mine, axsend.at[step], axrecv.at[step], x_peer(step))

    def act_x_wait(step):
        here = acts.at[core, lax.rem(x + 4 - step, 4)]
        remote(here, here, axsend.at[step], axrecv.at[step], x_peer(step)).wait_recv()

    def act_m(where, of_core):
        ref = acts.at[of_core, where]
        return remote(ref, ref, amsend.at[where], amrecv.at[where], mate)

    for slot in range(3):
        act_y(slot).start()

    def chunk(where, of_line, columns):
        return panel[pl.ds(where * 4 + 2 * of_line, 2), :, columns].reshape(64, columns.size)

    def wide_send(where, of_line):
        return remote(
            wide.at[where, of_line], wide_in.at[col, of_line],
            rsend.at[where, of_line], rrecv.at[col, of_line], (row, where),
        )

    def slim_send(where, of_line):
        return remote(
            slim.at[where, of_line], slim_in.at[col, of_line],
            rsend.at[where, of_line], rrecv.at[col, of_line], (row, where),
        )

    def input_grad(pieces):
        pieces = [(where, 1 - line if of_partner else line) for where, of_partner in pieces]

        lhs = jnp.concatenate([chunk(*piece, pl.ds(0, 4 * quarter)) for piece in pieces], axis=0)
        total = lax.dot_general(
            lhs, w_v[...], (((1,), (1,)), ((), ())), preferred_element_type=F32
        )
        for i, (where, of_line) in enumerate(pieces):
            value = total[i * 64:(i + 1) * 64]
            same = lax.rem(where, 2) == side

            @pl.when(same)
            def _():
                wide[where, of_line] = value

            @pl.when(same & (where != col))
            def _():
                wide_send(where, of_line).start()

            @pl.when(jnp.logical_not(same))
            def _():
                slim[where, of_line] = value.astype(BF16)
                slim_send(where, of_line).start()

    def weight_grad(planes):
        def lhs_of(of_core, of_line):
            return jnp.concatenate(
                [acts[of_core, where // 2, 2 * lax.rem(where, 2) + of_line] for where in planes], axis=1
            )

        def rhs_of(columns):
            return jnp.concatenate(
                [panel[pl.ds(where * 4, 4), :, columns].reshape(128, columns.size) for where in planes],
                axis=0,
            )

        def own(t, carry):
            columns = pl.ds(pl.multiple_of(t * quarter, quarter), quarter)
            out = jnp.dot(lhs_of(core, line), rhs_of(columns), preferred_element_type=F32)
            wg_ref[:, columns] = out.astype(BF16)
            return carry

        lax.fori_loop(0, 4, own, 0)

        def others(t, carry):
            which = lax.rem(member + 1 + t, 4)
            columns = pl.ds(pl.multiple_of(member * quarter, quarter), quarter)
            out = jnp.dot(
                lhs_of(lax.rem(which, 2), which // 2), rhs_of(columns), preferred_element_type=F32
            )
            g_ref[which] = out.astype(BF16)
            return carry

        lax.fori_loop(0, 3, others, 0)

    def pair(step):
        return [plane(step, 0), plane(step, 1)]

    def from_z(of_partner, step, which):
        for way in range(2):
            zwait(of_partner, step, way, which)
            if step < 3:
                zcopy(of_partner, step + 1, way, which).start()
            elif step == 3 and not of_partner and way == which:
                zcopy(False, 4, way, which).start()
            if step == 1:
                ycopy(1 + way, which).start()
            hand(plane(step, way), of_partner, which)

    def from_y_near(which):
        for way in range(2):
            ywait(1 + way, which)
            zcopy(True, 2, way, which).start()
            hand(plane(1, way), True, which)

    from_z(False, 1, 0)
    from_z(False, 1, 1)
    for which in range(2):
        ywait(0, which)
        hand(z, True, which)
    for slot in range(3):
        act_y_wait(slot)
    for step in range(1, 4):
        act_x(step).start()
    act_m(x, core).start()
    from_z(False, 2, 0)
    own_copy.wait()
    w_copy.wait()
    from_mate(z, False)
    from_z(False, 2, 1)
    from_mate(z, True)
    input_grad([(z, False), (z, True)])
    from_z(False, 3, 0)
    from_y_near(0)
    for where in pair(1):
        from_mate(where, False)
    input_grad([(where, False) for where in pair(1)])
    from_z(False, 3, 1)
    from_y_near(1)
    for where in pair(2):
        from_mate(where, False)
    input_grad([(where, False) for where in pair(2)])
    for way in range(2):
        zwait(False, 4, way, way)
        ycopy(3, way).start()
        hand(plane(4, 0), False, way)
    for where in pair(1):
        from_mate(where, True)
    input_grad([(where, True) for where in pair(1)])
    from_z(True, 2, 0)
    for where in pair(3):
        from_mate(where, False)
    from_mate(plane(4, 0), False)
    input_grad([(where, False) for where in pair(3)] + [(plane(4, 0), False)])
    from_z(True, 2, 1)
    for step in range(1, 4):
        act_x_wait(step)
        act_m(lax.rem(x + 4 - step, 4), core).start()
    for where in pair(2):
        from_mate(where, True)
    input_grad([(where, True) for where in pair(2)])
    for which in range(2):
        ywait(3, which)
        hand(plane(4, 0), True, which)
    from_z(True, 3, 0)
    from_z(True, 3, 1)
    for where in pair(3):
        from_mate(where, True)
    from_mate(plane(4, 0), True)
    input_grad([(where, True) for where in pair(3)] + [(plane(4, 0), True)])
    for where in range(4):
        act_m(where, 1 - core).wait_recv()
    weight_grad([z] + pair(1) + pair(2) + pair(3) + [plane(4, 0)])
    g_ref[member] = wg_ref[:, pl.ds(pl.multiple_of(member * quarter, quarter), quarter)]

    for of_line in range(2):
        rows = pl.ds(of_line * 64, 64)

        def take_wide(step, total):
            where = lax.rem(x + step, 4) * 2 + side
            ref = wide_in.at[where, of_line]
            remote(ref, ref, rsend.at[where, of_line], rrecv.at[where, of_line], (row, where)).wait_recv()
            return total + wide_in[where, of_line]

        def take_slim(step, total):
            where = lax.rem(x + step, 4) * 2 + 1 - side
            ref = slim_in.at[where, of_line]
            remote(ref, ref, rsend.at[where, of_line], rrecv.at[where, of_line], (row, where)).wait_recv()
            return total + slim_in[where, of_line].astype(F32)

        total = lax.fori_loop(1, 4, take_wide, wide[col, of_line])
        ig_ref[rows, :] = lax.fori_loop(0, 4, take_slim, total).astype(BF16)

    for way in range(2):
        for which in range(2):
            for step in range(1, 4):
                zcopy(False, step, way, which).wait_send()
            for step in range(2, 4):
                zcopy(True, step, way, which).wait_send()
        zcopy(False, 4, way, way).wait_send()
    for slot in range(4):
        for which in range(2):
            ycopy(slot, which).wait_send()
    for slot in range(3):
        act_y(slot).wait_send()
        act_x(slot + 1).wait_send()

    def drain(where, carry):
        for of_line in range(2):
            for which in range(2):
                mcopy(where, of_line, which, core).wait_send()
        return carry

    lax.fori_loop(0, 8, drain, 0)
    for where in range(4):
        act_m(where, core).wait_send()

    def drain_sums(step, carry):
        for of_line in range(2):
            @pl.when(step > 0)
            def _():
                wide_send(lax.rem(x + step, 4) * 2 + side, of_line).wait_send()

            slim_send(lax.rem(x + step, 4) * 2 + 1 - side, of_line).wait_send()
        return carry

    lax.fori_loop(0, 4, drain_sums, 0)


def gram_kernel(
    g_ref, wg_in, ig_in, left_ref, right_ref, wg_out, ig_out, left_v, right_v, sem
):
    size = g_ref.shape[0]
    step = size // 4
    scale = 1.0 / size
    copies = [
        pltpu.make_async_copy(wg_in, wg_out, sem.at[8]),
        pltpu.make_async_copy(ig_in, ig_out, sem.at[9]),
    ]
    for copy in copies:
        copy.start()
    for kind, (out_v, out_ref) in enumerate(((left_v, left_ref), (right_v, right_ref))):
        for i in range(4):
            low = i * step
            if kind == 0:
                out = lax.dot_general(
                    g_ref[low:low + step, :], g_ref[low:, :], (((1,), (1,)), ((), ())),
                    preferred_element_type=F32,
                )
            else:
                out = lax.dot_general(
                    g_ref[:, low:low + step], g_ref[:, low:], (((0,), (0,)), ((), ())),
                    preferred_element_type=F32,
                )
            out = out * scale
            out_v[low:low + step, low:] = out
            for j in range(i + 1, 4):
                block = out[:, (j - i) * step:(j - i + 1) * step]
                out_v[j * step:(j + 1) * step, low:low + step] = block.T
            rows = pl.ds(low, step)
            copy = pltpu.make_async_copy(out_v.at[rows], out_ref.at[rows], sem.at[kind * 4 + i])
            copy.start()
            copies.append(copy)
    for copy in copies:
        copy.wait()


def on_device(activations, out_grad, weight):
    tokens, feats = activations.shape
    rows, cols = weight.shape
    vmem = pl.BlockSpec(memory_space=pltpu.VMEM)
    anywhere = pl.BlockSpec(memory_space=pl.ANY)
    dma = pltpu.SemaphoreType.DMA
    quarter = cols // 4
    input_grad, weight_grad, blocks = pl.pallas_call(
        gather_kernel,
        out_shape=(
            jax.ShapeDtypeStruct((tokens, feats), BF16),
            jax.ShapeDtypeStruct((rows, cols), BF16),
            jax.ShapeDtypeStruct((4, rows, quarter), BF16),
        ),
        in_specs=[anywhere, anywhere, anywhere],
        out_specs=(vmem, vmem, vmem),
        scratch_shapes=[
            pltpu.VMEM((32, out_grad.shape[0], cols), BF16),
            pltpu.VMEM((rows, cols), BF16),
            pltpu.VMEM((tokens, feats), BF16),
            pltpu.VMEM((2, 4, 4, feats, tokens), BF16),
            pltpu.VMEM((8, 2, tokens // 2, feats), F32),
            pltpu.VMEM((8, 2, tokens // 2, feats), F32),
            pltpu.VMEM((8, 2, tokens // 2, feats), BF16),
            pltpu.VMEM((8, 2, tokens // 2, feats), BF16),
            dma((3,)),
            dma((2, 2, 4, 2)), dma((2, 2, 4, 2)), dma((4, 2)), dma((4, 2)), dma((16, 2)), dma((16, 2)),
            dma((3,)), dma((3,)), dma((4,)), dma((4,)), dma((4,)), dma((4,)), dma((8, 2)), dma((8, 2)),
        ],
        compiler_params=pltpu.CompilerParams(
            collective_id=0, has_side_effects=True, vmem_limit_bytes=44 * 2**20
        ),
        name="gather_and_grads",
    )(*[pltpu.with_memory_space_constraint(a, pltpu.HBM) for a in (activations, out_grad, weight)])

    size = 4 * rows
    left, right, weight_grad, input_grad = pl.pallas_call(
        gram_kernel,
        out_shape=(
            jax.ShapeDtypeStruct((size, quarter), F32),
            jax.ShapeDtypeStruct((quarter, quarter), F32),
            jax.ShapeDtypeStruct((rows, cols), BF16),
            jax.ShapeDtypeStruct((tokens, feats), BF16),
        ),
        in_specs=[vmem, vmem, vmem],
        out_specs=(anywhere,) * 4,
        scratch_shapes=[
            pltpu.VMEM((size, quarter), F32), pltpu.VMEM((quarter, quarter), F32), dma((10,)),
        ],
        compiler_params=pltpu.CompilerParams(vmem_limit_bytes=32 * 2**20),
        name="grams",
    )(blocks.reshape(size, quarter), weight_grad, input_grad)
    return (
        input_grad,
        weight_grad,
        left.reshape(1, 1, 1, size, quarter),
        right.reshape(1, 1, 1, quarter, quarter),
    )


def solution(mesh):
    return jax.shard_map(
        on_device,
        mesh=mesh,
        in_specs=(P("col", "row"), P("row", "col"), P("row", "col")),
        out_specs=(
            P("col", "row"),
            P("row", "col"),
            P("row", "col", None, None, None),
            P("row", "col", None, None, None),
        ),
        check_vma=False,
    )
```
